256 devices in a mesh: dp: 32 (over z, x_hi, core), group: 8 (over x_lo, y).
Axes of the slice: x: 4 (x_hi: 2, x_lo: 2; x = x_hi * 2 + x_lo), y: 4, z: 8, core: 2. Of those that a mesh axis runs over, the one named last changes fastest.
Arguments:
- img_feats: bfloat16 [114688, 1152], P(('dp', 'group')), may hold values from -6 to 6
- txt_feats: bfloat16 [114688, 1152], P(('dp', 'group')), may hold values from -6 to 6
- img_head: bfloat16 [1152, 1152], replicated, may hold values from -1 to 1
- txt_head: bfloat16 [1152, 1152], replicated, may hold values from -1 to 1
- log_temp: float32 [], replicated, may hold values from 2.3 to 3.4
- bias: float32 [], replicated, may hold values from -3 to -1
Outputs:
- loss: float32 [], replicated
- grad_log_temp: float32 [], replicated
- grad_bias: float32 [], replicated
- grad_img_feats: bfloat16 [114688, 1152], P(('dp', 'group'))
- grad_txt_feats: bfloat16 [114688, 1152], P(('dp', 'group'))
- grad_img_head: float32 [1152, 1152], P('dp', 'group')
- grad_txt_head: float32 [1152, 1152], P('dp', 'group')
The draws below stay inside these ranges and needn't reach their ends.
All inputs are finite; a program needn't handle non-finite values.
Results may differ from the reference program's by a relative error of at most 0.0045.
Values may be sent and summed in bfloat16 or wider, within the bound.
No kernel may reach another device: no remote copies, remote signals or barrier semaphores. Data moves between devices by JAX's collectives and lax.ppermute only.
A program may use at most 128 MiB of HBM per device.

```python
import jax
import jax.numpy as jnp
from jax import lax

D = 1152
TOK_DEV = 448
ROUNDS = 2
TOKENS = 114688
N_DP = 32
N_GROUP = 8


def block_direction(key):
    blocks = TOKENS // TOK_DEV
    table = jax.random.normal(key, (blocks, D), jnp.float32)
    return jnp.repeat(table, TOK_DEV, axis=0, total_repeat_length=TOKENS)


def shared_head(key):
    return jax.random.normal(key, (D, D), jnp.float32)


def block_position(key):
    blocks = TOKENS // TOK_DEV
    where = (jnp.arange(TOKENS) // TOK_DEV).astype(jnp.float32)
    return where / max(blocks - 1, 1)


def draw_img_feats(key, part):
    direction = block_direction(key)
    place = block_position(key)
    key = jax.random.fold_in(key, 11)
    first, second = jax.random.split(key)
    jitter = jax.random.uniform(second, (TOKENS, 1), jnp.float32, 0.8, 1.2)
    noise = jax.random.normal(first, (TOKENS, D), jnp.float32)
    strength = 0.15 + 0.85 * place
    values = noise + strength[:, None] * jitter * direction
    return jnp.clip(values, -6.0, 6.0).astype(jnp.bfloat16)


def draw_txt_feats(key, part):
    direction = block_direction(key)
    place = block_position(key)
    key = jax.random.fold_in(key, 23)
    first, second = jax.random.split(key)
    jitter = jax.random.uniform(second, (TOKENS, 1), jnp.float32, 0.8, 1.2)
    noise = jax.random.normal(first, (TOKENS, D), jnp.float32)
    strength = 0.15 + 0.85 * place
    values = noise + strength[:, None] * jitter * direction
    return jnp.clip(values, -6.0, 6.0).astype(jnp.bfloat16)


def draw_img_head(key, part):
    common = shared_head(jax.random.fold_in(key, 101))
    values = common * D ** (-0.5)
    return jnp.clip(values, -1.0, 1.0).astype(jnp.bfloat16)


def draw_txt_head(key, part):
    common = shared_head(jax.random.fold_in(key, 101))
    key = jax.random.fold_in(key, 41)
    own = jax.random.normal(key, (D, D), jnp.float32)
    values = (0.8 * common + 0.6 * own) * D ** (-0.5)
    return jnp.clip(values, -1.0, 1.0).astype(jnp.bfloat16)


def setup_inputs(seed: int = 0) -> dict:
    streams_of = jax.random.split(jax.random.key(seed), 7)
    return {
        "img_feats": draw_img_feats(jax.random.fold_in(streams_of[6], 71), 0),
        "txt_feats": draw_txt_feats(jax.random.fold_in(streams_of[6], 71), 0),
        "img_head": draw_img_head(jax.random.fold_in(streams_of[6], 71), 0),
        "txt_head": draw_txt_head(jax.random.fold_in(streams_of[6], 71), 0),
        "log_temp": jnp.clip(jax.random.uniform(streams_of[4], (), jnp.float32, 2.3, 3.4), 2.3, 3.4),
        "bias": jnp.clip(jax.random.uniform(streams_of[5], (), jnp.float32, -3.0, -1.0), -3.0, -1.0),
    }


def normed(feats, head):
    z = jnp.dot(feats, head, preferred_element_type=jnp.float32)
    n = jnp.sqrt(lax.optimization_barrier(jnp.sum(z * z, axis=-1, keepdims=True)) + 1e-06)
    return (z, n)

def pair_block(rows, cols, temp, bias, diagonal):
    dots = jnp.einsum('agkd,agjd->agkj', rows.astype(jnp.float32), cols.astype(jnp.float32))
    scaled = temp * dots
    logits = scaled + bias
    width = rows.shape[2]
    if diagonal:
        marker = jnp.eye(width, dtype=jnp.float32)
    else:
        marker = jnp.zeros((width, width), jnp.float32)
    terms = jax.nn.softplus(logits - 2.0 * marker * logits)
    grads = jax.nn.sigmoid(logits) - marker
    low = lax.optimization_barrier(grads.astype(jnp.bfloat16)).astype(jnp.float32)
    row_grad = temp * jnp.einsum('agkj,agjd->agkd', low, cols.astype(jnp.float32))
    col_grad = temp * jnp.einsum('agkj,agkd->agjd', low, rows.astype(jnp.float32))
    sums = (jnp.sum(terms), jnp.sum(grads), jnp.sum(grads * scaled))
    return (sums, row_grad, col_grad)

def rounded_back(piece, steps):
    low = lax.optimization_barrier(piece.astype(jnp.bfloat16))
    return jnp.roll(low, -steps, axis=0).astype(jnp.float32)

def reference(img_feats, txt_feats, img_head, txt_head, log_temp, bias):
    z_img, n_img = normed(img_feats, img_head)
    z_txt, n_txt = normed(txt_feats, txt_head)
    img_emb = (z_img / n_img).astype(jnp.bfloat16)
    txt_emb = (z_txt / n_txt).astype(jnp.bfloat16)
    temp = jnp.exp(log_temp)
    shape4 = (N_DP, N_GROUP, TOK_DEV, D)
    img4 = img_emb.reshape(shape4)
    txt4 = txt_emb.reshape(shape4)
    sums, grad_u, grad_v = pair_block(img4, txt4, temp, bias, True)
    total, gsum, glsum = sums
    for steps in range(1, ROUNDS + 1):
        txt_low = jnp.roll(txt4, steps, axis=0)
        img_low = jnp.roll(img4, steps, axis=0)
        sums_a, row_a, col_a = pair_block(img4, txt_low, temp, bias, False)
        sums_b, row_b, col_b = pair_block(img_low, txt4, temp, bias, False)
        grad_u = grad_u + row_a + rounded_back(row_b, steps)
        grad_v = grad_v + col_b + rounded_back(col_a, steps)
        total = total + sums_a[0] + sums_b[0]
        gsum = gsum + sums_a[1] + sums_b[1]
        glsum = glsum + sums_a[2] + sums_b[2]
    count = TOKENS * TOK_DEV * (2 * ROUNDS + 1)
    loss = total / count
    grad_bias = gsum / count
    grad_log_temp = glsum / count
    grad_u = grad_u.reshape(TOKENS, D)
    grad_v = grad_v.reshape(TOKENS, D)
    unit_img = z_img / n_img
    unit_txt = z_txt / n_txt
    dz_img = ((grad_u - unit_img * lax.optimization_barrier(jnp.sum(unit_img * grad_u, axis=-1, keepdims=True))) / n_img).astype(jnp.bfloat16)
    dz_txt = ((grad_v - unit_txt * lax.optimization_barrier(jnp.sum(unit_txt * grad_v, axis=-1, keepdims=True))) / n_txt).astype(jnp.bfloat16)
    grad_img_feats = jnp.dot(dz_img, img_head.T, preferred_element_type=jnp.float32).astype(jnp.bfloat16)
    grad_txt_feats = jnp.dot(dz_txt, txt_head.T, preferred_element_type=jnp.float32).astype(jnp.bfloat16)
    grad_img_head = jnp.dot(img_feats.T, dz_img, preferred_element_type=jnp.float32)
    grad_txt_head = jnp.dot(txt_feats.T, dz_txt, preferred_element_type=jnp.float32)
    return (loss, grad_log_temp, grad_bias, grad_img_feats, grad_txt_feats, grad_img_head, grad_txt_head)
```

```python
import functools

import jax
import jax.numpy as jnp
import numpy as np
from jax import lax
from jax.experimental import pallas as pl
from jax.experimental.pallas import tpu as pltpu
from jax.sharding import Mesh
from jax.sharding import PartitionSpec as P

AXES = ("z", "xh", "core", "xl", "y")
SIZES = (8, 2, 2, 2, 4)
ROUNDS = 2
ROWS = 448
D = 1152
CHUNKS = 2
CH = ROWS // CHUNKS
GC = 144
RC = 288
PC = 36
SV = 16
F32 = jnp.float32
BF16 = jnp.bfloat16
NT = (((1,), (1,)), ((), ()))
TN = (((0,), (0,)), ((), ()))


def permutation(move):
    pairs = []
    for source in range(int(np.prod(SIZES))):
        z, xh, core, xl, y = (int(i) for i in np.unravel_index(source, SIZES))
        place = {"z": z, "x": xh * 2 + xl, "y": y, "core": core}
        place = {**place, **move(place)}
        x = place["x"] % 4
        target = (place["z"] % 8, x // 2, place["core"] % 2, x % 2, place["y"] % 4)
        pairs.append((source, int(np.ravel_multi_index(target, SIZES))))
    return pairs


def send(value, move):
    return lax.ppermute(value, AXES, permutation(move))


def to_partner(p):
    return {"x": p["x"] + 2}


def onward(p):
    return {"z": p["z"] + (1 if p["x"] < 2 else -1)}


def to_sibling(p):
    return {"core": p["core"] + 1}


def first_axis(by):
    return lambda p: {"y": p["y"] + by} if p["core"] == 0 else {"x": p["x"] + by}


def second_axis(by):
    return lambda p: {"x": p["x"] + by} if p["core"] == 0 else {"y": p["y"] + by}


VMEM = pl.BlockSpec(memory_space=pltpu.VMEM)
SMEM = pl.BlockSpec(memory_space=pltpu.SMEM)


def call(kernel, inputs, outputs, flops, name, scalars=1, limit=48):
    size = sum(int(np.prod(a.shape)) * a.dtype.itemsize for a in [*inputs, *outputs])
    return pl.pallas_call(
        kernel,
        out_shape=tuple(outputs),
        in_specs=[SMEM] * scalars + [VMEM] * (len(inputs) - scalars),
        out_specs=tuple(VMEM for _ in outputs),
        compiler_params=pltpu.CompilerParams(vmem_limit_bytes=limit * 1024 * 1024),
        cost_estimate=pl.CostEstimate(flops=flops, bytes_accessed=size, transcendentals=0),
        name=name,
    )(*inputs)


def out(shape, dtype):
    return jax.ShapeDtypeStruct(shape, dtype)


def embed_kernel(feats, head, emb, unit, norm, *parts):
    z = jnp.dot(feats[...], head[...], preferred_element_type=F32)
    n = jnp.sqrt(jnp.sum(z * z, axis=-1, keepdims=True) + 1e-06)
    e = z / n
    unit[...] = e
    norm[...] = n
    low = e.astype(BF16)
    emb[...] = low
    for i, part in enumerate(parts):
        part[...] = low[i * CH : (i + 1) * CH]


def embed(feats, head):
    got = call(
        embed_kernel,
        [feats, head],
        [out((ROWS, D), BF16), out((ROWS, D), F32), out((ROWS, 1), F32)]
        + [out((CH, D), BF16)] * CHUNKS,
        2 * ROWS * D * D,
        "embed",
        scalars=0,
    )
    return got[0], got[1], got[2], list(got[3:])


def pair_kernel(blocks, own, stats, more, *refs):
    refs = list(refs)
    scale = refs.pop(0)
    emb = refs.pop(0)
    cols = [refs.pop(0) for _ in range(blocks)]
    before = [refs.pop(0) for _ in range((2 if stats else 1) if more else 0)]
    total_out = refs.pop(0)
    temp, bias = scale[0], scale[1]
    rows = emb[...]
    total = before[0][...] if more else None
    sums = before[1][...] if more and stats else None
    for i, ref in enumerate(cols):
        block = ref[...]
        scaled = temp * lax.dot_general(rows, block, NT, preferred_element_type=F32)
        logits = scaled + bias
        small = jnp.exp(-jnp.abs(logits))
        inverse = 1.0 / (1.0 + small)
        grads = jnp.where(logits >= 0, inverse, small * inverse)
        mark = None
        if own and i == 0:
            shape = logits.shape
            mark = lax.broadcasted_iota(jnp.int32, shape, 0) == lax.broadcasted_iota(
                jnp.int32, shape, 1
            )
            grads = jnp.where(mark, grads - 1.0, grads)
        if stats:
            signed = logits if mark is None else jnp.where(mark, -logits, logits)
            terms = jnp.maximum(signed, 0.0) + jnp.log1p(small)
            width = logits.shape[1]
            three = [
                jnp.sum(v, axis=0, keepdims=True) for v in (terms, grads, grads * scaled)
            ]
            tile = jnp.concatenate([*three, jnp.zeros((5, width), F32)], axis=0)
            if width < ROWS:
                tile = jnp.concatenate([tile, jnp.zeros((8, ROWS - width), F32)], axis=1)
            sums = tile if sums is None else sums + tile
        part = jnp.dot(grads.astype(BF16), block, preferred_element_type=F32)
        total = part if total is None else total + part
    total_out[...] = total
    if stats:
        refs[0][...] = sums


def pairs(scale, emb, cols, state, own, stats, name):
    n = sum(c.shape[0] for c in cols)
    got = call(
        functools.partial(pair_kernel, len(cols), own, stats, state is not None),
        [scale, emb, *cols, *(state or ())],
        [out((ROWS, D), F32)] + ([out((8, ROWS), F32)] if stats else []),
        4 * ROWS * n * D,
        name,
    )
    return tuple(got)


def three_parts(value):
    high = value.astype(BF16).astype(F32)
    rest = value - high
    middle = rest.astype(BF16).astype(F32)
    lane = lax.broadcasted_iota(jnp.int32, (SV, RC), 1)
    parts = jnp.where(lane == 0, high, jnp.where(lane == 1, middle, jnp.where(lane == 2, rest - middle, 0.0)))
    return parts.astype(BF16)


def joined(rows):
    return jnp.sum(rows.astype(F32), axis=1, keepdims=True)


def tangent_kernel(scale, place, total, unit, norm, feats, sums, dz, message, scalars):
    grad = scale[0] * total[...]
    e = unit[...]
    along = jnp.sum(e * grad, axis=-1, keepdims=True)
    low = ((grad - e * along) / norm[...]).astype(BF16)
    dz[...] = low
    core = place[0]
    for half in range(2):
        part = lax.dot_general(low, feats[(1 - core) * 2 + half], TN, preferred_element_type=F32)
        message[half * D : (half + 1) * D] = part.astype(BF16)
    value = jnp.sum(sums[...], axis=1, keepdims=True)
    value = jnp.concatenate([value, jnp.zeros((SV - 8, 1), F32)], axis=0)
    scalars[...] = value
    message[2 * D :] = three_parts(value)


def tangent(scale, place, total, unit, norm, feats, sums):
    return call(
        tangent_kernel,
        [scale, place, total, unit, norm, feats, sums],
        [out((ROWS, D), BF16), out((2 * D + SV, RC), BF16), out((SV, 1), F32)],
        2 * ROWS * D * D // 2,
        "tangent",
        scalars=2,
    )


def keep_kernel(place, dz, feats, kept):
    core = place[0]
    for half in range(2):
        kept[half * D : (half + 1) * D] = lax.dot_general(
            dz[...], feats[core * 2 + half], TN, preferred_element_type=F32
        )


def keep(place, dz, feats):
    return call(keep_kernel, [place, dz, feats], [out((2 * D, RC), F32)], ROWS * D * D, "keep")[0]


def back_kernel(dz, head, grad):
    grad[...] = lax.dot_general(dz[...], head[...], NT, preferred_element_type=F32).astype(BF16)


def back(dz, head):
    return call(
        back_kernel, [dz, head], [out((ROWS, D), BF16)], 2 * ROWS * D * D, "back", scalars=0
    )[0]


def first_kernel(place, kept, got, scalars, own, own_scalars, *messages):
    core, x, y = place[0], place[1], place[2]
    mine = jnp.where(core == 0, y, x)

    def block(t, u):
        number = jnp.where(core == 0, u * 4 + t, t * 4 + u)
        rows = pl.ds(pl.multiple_of(number * GC, GC), GC)
        return kept[rows] + got[rows].astype(F32)

    value = scalars[...] + joined(got[2 * D :])
    own_scalars[...] = value
    parts = three_parts(value)
    for by, message in enumerate(messages, 1):
        t = lax.rem(mine + by, 4)
        for u in range(4):
            message[u * GC : (u + 1) * GC] = block(t, u).astype(BF16)
        message[4 * GC :] = parts
    for u in range(4):
        own[u * GC : (u + 1) * GC] = block(mine, u)


def second_kernel(place, own, scalars, one, two, three, mine, own_scalars, *messages):
    core, x, y = place[0], place[1], place[2]
    other = jnp.where(core == 0, x, y)

    def block(u):
        rows = pl.ds(pl.multiple_of(u * GC, GC), GC)
        return (own[rows] + one[rows].astype(F32)) + (
            two[rows].astype(F32) + three[rows].astype(F32)
        )

    value = scalars[...]
    for ref in (one, two, three):
        value = value + joined(ref[4 * GC :])
    own_scalars[...] = value
    parts = three_parts(value)
    for by, message in enumerate(messages, 1):
        message[:GC] = block(lax.rem(other + by, 4)).astype(BF16)
        message[GC:] = parts
    mine[...] = block(other)


def third_kernel(own, scalars, one, two, three, pieces):
    total = (own[...] + one[:GC].astype(F32)) + (
        two[:GC].astype(F32) + three[:GC].astype(F32)
    )
    value = scalars[...]
    for ref in (one, two, three):
        value = value + joined(ref[GC:])
    turned = total.T
    lane = lax.broadcasted_iota(jnp.int32, (4, GC), 1)
    row = lax.broadcasted_iota(jnp.int32, (4, GC), 0)
    tail = jnp.zeros((4, GC), F32)
    for i in range(3):
        tail = jnp.where((row == i) & (lane == 0), value[i : i + 1], tail)
    for i in range(8):
        pieces[i, :PC] = turned[i * PC : (i + 1) * PC]
        pieces[i, PC:] = tail


def reduced(place, dz, feats, message, scalars):
    got = send(message, to_sibling)
    kept = keep(place, dz, feats)
    own, scalars, *messages = call(
        first_kernel,
        [place, kept, got, scalars],
        [out((4 * GC, RC), F32), out((SV, 1), F32)] + [out((4 * GC + SV, RC), BF16)] * 3,
        0,
        "first",
    )
    got = [send(m, first_axis(by)) for by, m in enumerate(messages, 1)]
    own, scalars, *messages = call(
        second_kernel,
        [place, own, scalars, *got],
        [out((GC, RC), F32), out((SV, 1), F32)] + [out((GC + SV, RC), BF16)] * 3,
        0,
        "second",
    )
    got = [send(m, second_axis(by)) for by, m in enumerate(messages, 1)]
    (pieces,) = call(
        third_kernel,
        [own, scalars, *got],
        [out((8, PC + 4, GC), F32)],
        0,
        "third",
        scalars=0,
    )
    pieces = lax.all_to_all(pieces, "z", 0, 0)
    return jnp.sum(pieces, axis=0)


def local(img_feats, txt_feats, img_head, txt_head, log_temp, bias):
    core, xh = lax.axis_index("core"), lax.axis_index("xh")
    x = xh * 2 + lax.axis_index("xl")
    place = jnp.stack([core, x, lax.axis_index("y")]).astype(jnp.int32)
    scale = jnp.stack([jnp.exp(log_temp), bias])

    j = np.arange(RC)
    order = np.stack(
        [(j // PC) * 4 * PC + h * 2 * PC + c * PC + j % PC for c in range(2) for h in range(2)]
    )
    pick = jnp.arange(D)[None, :, None] == jnp.asarray(order)[:, None, :]
    pick = pick.astype(BF16)

    def ordered(feats):
        return jnp.einsum("rd,kdj->krj", feats, pick, preferred_element_type=F32).astype(BF16)

    def exchanged(parts):
        near = [send(p, to_partner) for p in parts]
        far = [send(p, onward) for p in near]
        fourth = [
            send(jnp.where(xh == core, a, b), to_sibling) for a, b in zip(near, far, strict=True)
        ]
        return near, far, fourth

    txt_emb, txt_unit, txt_norm, txt_parts = embed(txt_feats, txt_head)
    img_emb, img_unit, img_norm, img_parts = embed(img_feats, img_head)

    near, far, fourth = exchanged(txt_parts)
    sibling = send(txt_emb, to_sibling)
    near_img, far_img, fourth_img = exchanged(img_parts)
    sibling_img = send(img_emb, to_sibling)

    img_rows, txt_rows = ordered(img_feats), ordered(txt_feats)

    state = pairs(scale, img_emb, [txt_emb, sibling], None, True, True, "own_a")
    for a, b, c in zip(near, far, fourth, strict=True):
        state = pairs(scale, img_emb, [a], state, False, True, "near_a")
        state = pairs(scale, img_emb, [b, c], state, False, True, "far_a")
    dz, message, scalars = tangent(scale, place, state[0], img_unit, img_norm, img_rows, state[1])
    img_sum = reduced(place, dz, img_rows, message, scalars)
    grad_img_feats = back(dz, img_head)

    state = pairs(scale, txt_emb, [img_emb, sibling_img], None, True, False, "own_b")
    for a, b, c in zip(near_img, far_img, fourth_img, strict=True):
        state = pairs(scale, txt_emb, [a], state, False, False, "near_b")
        state = pairs(scale, txt_emb, [b, c], state, False, False, "far_b")
    none = jnp.zeros((8, ROWS), F32)
    dz, message, scalars = tangent(scale, place, state[0], txt_unit, txt_norm, txt_rows, none)
    txt_sum = reduced(place, dz, txt_rows, message, scalars)
    grad_txt_feats = back(dz, txt_head)

    count = int(np.prod(SIZES)) * ROWS * ROWS * (2 * ROUNDS + 1)
    loss, grad_bias, grad_log_temp = (img_sum[PC + i, 0] / count for i in range(3))
    return (
        loss,
        grad_log_temp,
        grad_bias,
        grad_img_feats,
        grad_txt_feats,
        img_sum[:PC],
        txt_sum[:PC],
    )


def solution(mesh):
    fine = Mesh(mesh.devices.reshape(SIZES), AXES)
    rows = P(AXES, None)
    tile = P(AXES[:3], AXES[3:])
    return jax.shard_map(
        local,
        mesh=fine,
        in_specs=(rows, rows, P(), P(), P(), P()),
        out_specs=(P(), P(), P(), rows, rows, tile, tile),
        check_vma=False,
    )
```

```python
import functools

import jax
import jax.numpy as jnp
import numpy as np
from jax import lax
from jax.experimental import pallas as pl
from jax.experimental.pallas import tpu as pltpu
from jax.sharding import Mesh
from jax.sharding import PartitionSpec as P

AXES = ("z", "xh", "core", "xl", "y")
SIZES = (8, 2, 2, 2, 4)
ROUNDS = 2
TAIL = 8
ROWS = 448
D = 1152
CHUNKS = 2
CH = ROWS // CHUNKS
GC = 144
RC = 288
RW = 384
PC = 36
SV = 16
COUNT = 256 * ROWS * ROWS * (2 * ROUNDS + 1)
F32 = jnp.float32
BF16 = jnp.bfloat16
NT = (((1,), (1,)), ((), ()))
TN = (((0,), (0,)), ((), ()))


def permutation(move):
    pairs = []
    for source in range(int(np.prod(SIZES))):
        z, xh, core, xl, y = (int(i) for i in np.unravel_index(source, SIZES))
        place = {"z": z, "x": xh * 2 + xl, "y": y, "core": core}
        place = {**place, **move(place)}
        x = place["x"] % 4
        target = (place["z"] % 8, x // 2, place["core"] % 2, x % 2, place["y"] % 4)
        pairs.append((source, int(np.ravel_multi_index(target, SIZES))))
    return pairs


def send(value, move):
    return lax.ppermute(value, AXES, permutation(move))


def to_partner(p):
    return {"x": p["x"] + 2}


def onward(p):
    return {"z": p["z"] + (1 if p["x"] < 2 else -1)}


def to_sibling(p):
    return {"core": p["core"] + 1}


def first_axis(by):
    return lambda p: {"y": p["y"] + by} if p["core"] == 0 else {"x": p["x"] + by}


def second_axis(by):
    return lambda p: {"x": p["x"] + by} if p["core"] == 0 else {"y": p["y"] + by}


VMEM = pl.BlockSpec(memory_space=pltpu.VMEM)
SMEM = pl.BlockSpec(memory_space=pltpu.SMEM)


def call(kernel, inputs, outputs, flops, name, scalars=1, limit=24):
    size = sum(int(np.prod(a.shape)) * a.dtype.itemsize for a in [*inputs, *outputs])
    return pl.pallas_call(
        kernel,
        out_shape=tuple(outputs),
        in_specs=[SMEM] * scalars + [VMEM] * (len(inputs) - scalars),
        out_specs=tuple(VMEM for _ in outputs),
        compiler_params=pltpu.CompilerParams(vmem_limit_bytes=limit * 1024 * 1024),
        cost_estimate=pl.CostEstimate(flops=flops, bytes_accessed=size, transcendentals=0),
        name=name,
    )(*inputs)


def out(shape, dtype):
    return jax.ShapeDtypeStruct(shape, dtype)


def embed_kernel(start, feats, head, emb, unit, norm):
    z = jnp.dot(feats[start : start + CH], head[...], preferred_element_type=F32)
    n = jnp.sqrt(jnp.sum(z * z, axis=-1, keepdims=True) + 1e-06)
    e = z * (1.0 / n)
    unit[...] = e
    norm[...] = n
    emb[...] = e.astype(BF16)


def embed(feats, head, start, name):
    n = CH
    return call(
        functools.partial(embed_kernel, start),
        [feats, head],
        [out((n, D), BF16), out((n, D), F32), out((n, 1), F32)],
        2 * n * D * D,
        name,
        scalars=0,
    )


def whole(refs):
    values = [r[...] for r in refs]
    return values[0] if len(values) == 1 else jnp.concatenate(values, axis=0)


def pair_kernel(rows_in, blocks, own, stats, more, *refs):
    refs = list(refs)
    scale = refs.pop(0)
    rows = whole([refs.pop(0) for _ in range(rows_in)])
    cols = [[refs.pop(0) for _ in range(n)] for n in blocks]
    before = [refs.pop(0) for _ in range((2 if stats else 1) if more else 0)]
    total_out = refs.pop(0)
    temp, bias = scale[0], scale[1]
    total = before[0][...] if more else None
    sums = before[1][...] if more and stats else None
    for i, group in enumerate(cols):
        block = whole(group)
        scaled = temp * lax.dot_general(rows, block, NT, preferred_element_type=F32)
        logits = scaled + bias
        small = jnp.exp(-jnp.abs(logits))
        inverse = 1.0 / (1.0 + small)
        grads = jnp.where(logits >= 0, inverse, small * inverse)
        mark = None
        if own and i == 0:
            shape = logits.shape
            mark = lax.broadcasted_iota(jnp.int32, shape, 0) == lax.broadcasted_iota(
                jnp.int32, shape, 1
            )
            grads = jnp.where(mark, grads - 1.0, grads)
        if stats:
            signed = logits if mark is None else jnp.where(mark, -logits, logits)
            terms = jnp.maximum(signed, 0.0) + jnp.log1p(small)
            width = logits.shape[1]
            three = [
                jnp.sum(v, axis=0, keepdims=True) for v in (terms, grads, grads * scaled)
            ]
            tile = jnp.concatenate([*three, jnp.zeros((5, width), F32)], axis=0)
            if width < ROWS:
                tile = jnp.concatenate([tile, jnp.zeros((8, ROWS - width), F32)], axis=1)
            sums = tile if sums is None else sums + tile
        part = jnp.dot(grads.astype(BF16), block, preferred_element_type=F32)
        total = part if total is None else total + part
    total_out[...] = total
    if stats:
        refs[0][...] = sums


def pairs(scale, emb, cols, state, own, stats, name):
    n = sum(c.shape[0] for group in cols for c in group)
    got = call(
        functools.partial(
            pair_kernel, len(emb), [len(g) for g in cols], own, stats, state is not None
        ),
        [scale, *emb, *(c for group in cols for c in group), *(state or ())],
        [out((ROWS, D), F32)] + ([out((8, ROWS), F32)] if stats else []),
        4 * ROWS * n * D,
        name,
    )
    return tuple(got)


def choose_kernel(place, one, two, chosen):
    @pl.when(place[3] == 1)
    def _():
        chosen[...] = one[...]

    @pl.when(place[3] == 0)
    def _():
        chosen[...] = two[...]


def choose(place, one, two):
    return call(choose_kernel, [place, one, two], [out(one.shape, BF16)], 0, "choose")[0]


def order_kernel(feats, rows):
    values = feats[...]
    row = lax.broadcasted_iota(jnp.int32, (D, RW), 0)
    col = lax.broadcasted_iota(jnp.int32, (D, RW), 1)
    wanted = jnp.where(col < RC, col + lax.div(col, PC) * (3 * PC), -D)
    for c in range(2):
        for h in range(2):
            pick = (row == wanted + (c * PC + h * 2 * PC)).astype(F32).astype(BF16)
            rows[c * 2 + h] = jnp.dot(values, pick, preferred_element_type=F32).astype(BF16)


def ordered(feats):
    return call(
        order_kernel, [feats], [out((4, ROWS, RW), BF16)], 2 * ROWS * D * D, "ordered", scalars=0
    )[0]


def three_parts(value):
    high = value.astype(BF16).astype(F32)
    rest = value - high
    middle = rest.astype(BF16).astype(F32)
    lane = lax.broadcasted_iota(jnp.int32, (SV, RW), 1)
    parts = jnp.where(lane == 0, high, jnp.where(lane == 1, middle, jnp.where(lane == 2, rest - middle, 0.0)))
    return parts.astype(BF16)


def joined(rows):
    return jnp.sum(rows.astype(F32), axis=1, keepdims=True)


def tangent_kernel(scale, place, total, unit0, unit1, norm0, norm1, feats, sums, dz, message, scalars):
    core = place[0]
    lows = []
    for i, (unit, norm) in enumerate(((unit0, norm0), (unit1, norm1))):
        grad = scale[0] * total[i * CH : (i + 1) * CH]
        e = unit[...]
        along = jnp.sum(e * grad, axis=-1, keepdims=True)
        lows.append(((grad - e * along) * (1.0 / norm[...])).astype(BF16))
    low = jnp.concatenate(lows, axis=0)
    dz[...] = low
    for half in range(2):
        part = lax.dot_general(low, feats[(1 - core) * 2 + half], TN, preferred_element_type=F32)
        message[half * D : (half + 1) * D] = part.astype(BF16)
    value = jnp.sum(sums[...], axis=1, keepdims=True)
    value = jnp.concatenate([value, jnp.zeros((SV - 8, 1), F32)], axis=0)
    scalars[...] = value
    message[2 * D :] = three_parts(value)


def tangent(scale, place, total, unit, norm, feats, sums):
    return call(
        tangent_kernel,
        [scale, place, total, *unit, *norm, feats, sums],
        [out((ROWS, D), BF16), out((2 * D + SV, RW), BF16), out((SV, 1), F32)],
        2 * ROWS * D * D // 2,
        "tangent",
        scalars=2,
    )


def keep_kernel(place, dz, feats, kept):
    core = place[0]
    for half in range(2):
        kept[half * D : (half + 1) * D] = lax.dot_general(
            dz[...], feats[core * 2 + half], TN, preferred_element_type=F32
        )


def keep(place, dz, feats):
    return call(keep_kernel, [place, dz, feats], [out((2 * D, RW), F32)], ROWS * D * D, "keep")[0]


def back_kernel(dz, head, grad):
    grad[...] = lax.dot_general(dz[...], head[...], NT, preferred_element_type=F32).astype(BF16)


def back(dz, head):
    return call(
        back_kernel, [dz, head], [out((ROWS, D), BF16)], 2 * ROWS * D * D, "back", scalars=0
    )[0]


def first_kernel(place, kept, got, scalars, own, own_scalars, *messages):
    core, x, y = place[0], place[1], place[2]
    mine = jnp.where(core == 0, y, x)

    def block(t, u):
        number = jnp.where(core == 0, u * 4 + t, t * 4 + u)
        rows = pl.ds(pl.multiple_of(number * GC, GC), GC)
        return kept[rows] + got[rows].astype(F32)

    value = scalars[...] + joined(got[2 * D :])
    own_scalars[...] = value
    parts = three_parts(value)
    for by, message in enumerate(messages, 1):
        t = lax.rem(mine + by, 4)
        for u in range(4):
            message[u * GC : (u + 1) * GC] = block(t, u).astype(BF16)
        message[4 * GC :] = parts
    for u in range(4):
        own[u * GC : (u + 1) * GC] = block(mine, u)


def second_kernel(place, own, scalars, one, two, three, mine, own_scalars, *messages):
    core, x, y = place[0], place[1], place[2]
    other = jnp.where(core == 0, x, y)

    def block(u):
        rows = pl.ds(pl.multiple_of(u * GC, GC), GC)
        return (own[rows] + one[rows].astype(F32)) + (
            two[rows].astype(F32) + three[rows].astype(F32)
        )

    value = scalars[...]
    for ref in (one, two, three):
        value = value + joined(ref[4 * GC :])
    own_scalars[...] = value
    parts = three_parts(value)
    for by, message in enumerate(messages, 1):
        message[:GC] = block(lax.rem(other + by, 4)).astype(BF16)
        message[GC:] = parts
    mine[...] = block(other)


def third_kernel(own, scalars, one, two, three, turned, own_scalars):
    total = (own[...] + one[:GC].astype(F32)) + (
        two[:GC].astype(F32) + three[:GC].astype(F32)
    )
    value = scalars[...]
    for ref in (one, two, three):
        value = value + joined(ref[GC:])
    own_scalars[...] = value
    turned[...] = total.T[:RC]


def pieces_kernel(img, scalars, own, one, two, three, pieces):
    total = (own[...] + one[:GC].astype(F32)) + (
        two[:GC].astype(F32) + three[:GC].astype(F32)
    )
    tail = three_parts(scalars[...])[: TAIL, :GC]
    for i in range(8):
        rows = slice(i * PC, (i + 1) * PC)
        both = jnp.concatenate([img[rows], total.T[rows], tail.astype(F32)], axis=0)
        pieces[i] = both.astype(BF16)


def last_kernel(got, img, txt, scalars):
    total = got[0].astype(F32)
    for i in range(1, 8):
        total = total + got[i].astype(F32)
    img[...] = total[:PC]
    txt[...] = total[PC : 2 * PC]
    scalars[...] = jnp.sum(total[2 * PC :], axis=1, keepdims=True) / COUNT


def first(place, kept, got, scalars):
    own, scalars, *messages = call(
        first_kernel,
        [place, kept, got, scalars],
        [out((4 * GC, RW), F32), out((SV, 1), F32)] + [out((4 * GC + SV, RW), BF16)] * 3,
        0,
        "first",
    )
    return own, scalars, [send(m, first_axis(by)) for by, m in enumerate(messages, 1)]


def second(place, own, scalars, got):
    own, scalars, *messages = call(
        second_kernel,
        [place, own, scalars, *got],
        [out((GC, RW), F32), out((SV, 1), F32)] + [out((GC + SV, RW), BF16)] * 3,
        0,
        "second",
    )
    return own, scalars, [send(m, second_axis(by)) for by, m in enumerate(messages, 1)]


def third(own, scalars, got):
    return call(
        third_kernel,
        [own, scalars, *got],
        [out((RC, GC), F32), out((SV, 1), F32)],
        0,
        "third",
        scalars=0,
    )


def across_z(img, scalars, own, got):
    (pieces,) = call(
        pieces_kernel,
        [img, scalars, own, *got],
        [out((8, 2 * PC + TAIL, GC), BF16)],
        0,
        "pieces",
        scalars=0,
    )
    return call(
        last_kernel,
        [lax.all_to_all(pieces, "z", 0, 0)],
        [out((PC, GC), F32), out((PC, GC), F32), out((TAIL, 1), F32)],
        0,
        "last",
        scalars=0,
    )


def after(done, *values):
    got = lax.optimization_barrier((*values, done))[: len(values)]
    return got[0] if len(values) == 1 else got


def local(img_feats, txt_feats, img_head, txt_head, log_temp, bias):
    core, xh = lax.axis_index("core"), lax.axis_index("xh")
    x = xh * 2 + lax.axis_index("xl")
    place = jnp.stack([core, x, lax.axis_index("y"), xh == core]).astype(jnp.int32)
    scale = jnp.stack([jnp.exp(log_temp), bias])

    feats = after((place, scale), txt_feats)
    t0, txt_unit0, txt_norm0 = embed(feats, txt_head, 0, "embed_t0")
    near_t0, sib_t0 = send(t0, to_partner), send(t0, to_sibling)
    t1, txt_unit1, txt_norm1 = embed(after(t0, feats), txt_head, CH, "embed_t1")
    near_t1, sib_t1 = send(t1, to_partner), send(t1, to_sibling)
    feats = after(t1, img_feats)
    i0, img_unit0, img_norm0 = embed(feats, img_head, 0, "embed_i0")
    near_i0, sib_i0 = send(i0, to_partner), send(i0, to_sibling)
    i1, img_unit1, img_norm1 = embed(after(i0, feats), img_head, CH, "embed_i1")
    near_i1, sib_i1 = send(i1, to_partner), send(i1, to_sibling)
    txt, img = [t0, t1], [i0, i1]
    txt_unit, txt_norm = [txt_unit0, txt_unit1], [txt_norm0, txt_norm1]
    img_unit, img_norm = [img_unit0, img_unit1], [img_norm0, img_norm1]

    a = pairs(scale, img, [txt, [sib_t0, sib_t1]], None, True, True, "own_a")
    img_rows = ordered(after(a[1], img_feats))
    near_t0 = after(img_rows, near_t0)
    far_t0 = send(near_t0, onward)
    a = pairs(scale, img, [[near_t0]], a, False, True, "near_a0")
    (b,) = pairs(after(a[1], scale), txt, [img, [sib_i0, sib_i1]], None, True, False, "own_b")
    txt_rows = ordered(after(b, txt_feats))
    near_t1 = after(txt_rows, near_t1)
    far_t1 = send(near_t1, onward)
    a = pairs(scale, img, [[near_t1]], a, False, True, "near_a1")
    last_t0 = send(choose(after(a[1], place), near_t0, far_t0), to_sibling)
    near_i0 = after(last_t0, near_i0)
    far_i0 = send(near_i0, onward)
    a = pairs(scale, img, [[far_t0, last_t0]], a, False, True, "far_a0")
    last_t1 = send(choose(after(a[1], place), near_t1, far_t1), to_sibling)
    (b,) = pairs(after(a[1], scale), txt, [[near_i0]], (b,), False, False, "near_b0")
    a = pairs(after(b, scale), img, [[far_t1, last_t1]], a, False, True, "far_a1")
    dz_img, message, scalars = tangent(scale, place, a[0], img_unit, img_norm, img_rows, a[1])
    got = send(message, to_sibling)
    kept = keep(place, dz_img, img_rows)
    near_i1 = after(kept, near_i1)
    far_i1 = send(near_i1, onward)
    last_i0 = send(choose(after(kept, place), near_i0, far_i0), to_sibling)
    own, scalars, got = first(after(last_i0, place), kept, got, scalars)
    (b,) = pairs(after(own, scale), txt, [[near_i1]], (b,), False, False, "near_b1")
    (b,) = pairs(scale, txt, [[far_i0, last_i0]], (b,), False, False, "far_b0")
    grad_img_feats = back(after(b, dz_img), img_head)
    last_i1 = send(choose(after(grad_img_feats, place), near_i1, far_i1), to_sibling)
    own, scalars, got = second(after(last_i1, place), own, scalars, got)
    (b,) = pairs(after(own, scale), txt, [[far_i1, last_i1]], (b,), False, False, "far_b1")
    none = jnp.zeros((8, ROWS), F32)
    dz_txt, message, no_scalars = tangent(scale, place, b, txt_unit, txt_norm, txt_rows, none)
    got_txt = send(message, to_sibling)
    kept = keep(place, dz_txt, txt_rows)
    img_turned, scalars = third(after(kept, own), scalars, got)
    own, no_scalars, got = first(after(img_turned, place), kept, got_txt, no_scalars)
    grad_txt_feats = back(after(own, dz_txt), txt_head)
    own, no_scalars, got = second(after(grad_txt_feats, place), own, no_scalars, got)
    grad_img_head, grad_txt_head, scalars = across_z(img_turned, scalars, own, got)
    loss, grad_bias, grad_log_temp = (scalars[i, 0] for i in range(3))
    return (
        loss,
        grad_log_temp,
        grad_bias,
        grad_img_feats,
        grad_txt_feats,
        grad_img_head,
        grad_txt_head,
    )


def solution(mesh):
    fine = Mesh(mesh.devices.reshape(SIZES), AXES)
    rows = P(AXES, None)
    tile = P(AXES[:3], AXES[3:])
    return jax.shard_map(
        local,
        mesh=fine,
        in_specs=(rows, rows, P(), P(), P(), P()),
        out_specs=(P(), P(), P(), rows, rows, tile, tile),
        check_vma=False,
    )
```

```python
import functools

import jax
import jax.numpy as jnp
import numpy as np
from jax import lax
from jax.experimental import pallas as pl
from jax.experimental.pallas import tpu as pltpu
from jax.sharding import Mesh
from jax.sharding import PartitionSpec as P

AXES = ("z", "xh", "core", "xl", "y")
SIZES = (8, 2, 2, 2, 4)
ROUNDS = 2
TAIL = 8
ROWS = 448
D = 1152
CHUNKS = 2
CH = ROWS // CHUNKS
GC = 144
RC = 288
RW = 384
PC = 36
SV = 16
COUNT = 256 * ROWS * ROWS * (2 * ROUNDS + 1)
COST = {"own_a": 30, "own_b": 30, "keep_img": 30, "near_b0": 30, "second": 16}
F32 = jnp.float32
BF16 = jnp.bfloat16
NT = (((1,), (1,)), ((), ()))
TN = (((0,), (0,)), ((), ()))


def permutation(move):
    pairs = []
    for source in range(int(np.prod(SIZES))):
        z, xh, core, xl, y = (int(i) for i in np.unravel_index(source, SIZES))
        place = {"z": z, "x": xh * 2 + xl, "y": y, "core": core}
        place = {**place, **move(place)}
        x = place["x"] % 4
        target = (place["z"] % 8, x // 2, place["core"] % 2, x % 2, place["y"] % 4)
        pairs.append((source, int(np.ravel_multi_index(target, SIZES))))
    return pairs


def send(value, move):
    return lax.ppermute(value, AXES, permutation(move))


def to_partner(p):
    return {"x": p["x"] + 2}


def onward(p):
    return {"z": p["z"] + (1 if p["x"] < 2 else -1)}


def to_sibling(p):
    return {"core": p["core"] + 1}


def first_axis(by):
    return lambda p: {"y": p["y"] + by} if p["core"] == 0 else {"x": p["x"] + by}


def second_axis(by):
    return lambda p: {"x": p["x"] + by} if p["core"] == 0 else {"y": p["y"] + by}


VMEM = pl.BlockSpec(memory_space=pltpu.VMEM)
SMEM = pl.BlockSpec(memory_space=pltpu.SMEM)


def call(kernel, inputs, outputs, flops, name, scalars=1, limit=24):
    size = sum(int(np.prod(a.shape)) * a.dtype.itemsize for a in [*inputs, *outputs])
    return pl.pallas_call(
        kernel,
        out_shape=tuple(outputs),
        in_specs=[SMEM] * scalars + [VMEM] * (len(inputs) - scalars),
        out_specs=tuple(VMEM for _ in outputs),
        compiler_params=pltpu.CompilerParams(vmem_limit_bytes=limit * 1024 * 1024),
        cost_estimate=pl.CostEstimate(flops=COST.get(name, 0) * 10**9, bytes_accessed=0, transcendentals=0),
        name=name,
    )(*inputs)


def out(shape, dtype):
    return jax.ShapeDtypeStruct(shape, dtype)


def embed_kernel(start, feats, head, *refs):
    z = jnp.dot(feats[start : start + CH], head[...], preferred_element_type=F32)
    n = jnp.sqrt(jnp.sum(z * z, axis=-1, keepdims=True) + 1e-06)
    e = z * (1.0 / n)
    low = e.astype(BF16)
    emb, unit, norm = refs[-3:] if start == 0 else refs[1:4]
    unit[...] = e
    norm[...] = n
    emb[...] = low
    if start:
        refs[4][:start] = refs[0][...]
        refs[4][start:] = low


def embed(feats, head, start, name, earlier=()):
    shapes = [out((CH, D), BF16), out((CH, D), F32), out((CH, 1), F32)]
    return call(
        functools.partial(embed_kernel, start),
        [feats, head, *earlier],
        shapes + [out((ROWS, D), BF16)] * len(earlier),
        2 * CH * D * D,
        name,
        scalars=0,
    )


def whole(refs):
    values = [r[...] for r in refs]
    return values[0] if len(values) == 1 else jnp.concatenate(values, axis=0)


def pair_kernel(rows_in, blocks, own, stats, more, *refs):
    refs = list(refs)
    scale = refs.pop(0)
    rows = whole([refs.pop(0) for _ in range(rows_in)])
    cols = [[refs.pop(0) for _ in range(n)] for n in blocks]
    before = [refs.pop(0) for _ in range((2 if stats else 1) if more else 0)]
    total_out = refs.pop(0)
    temp, bias = scale[0], scale[1]
    total = before[0][...] if more else None
    sums = before[1][...] if more and stats else None
    for i, group in enumerate(cols):
        block = whole(group)
        scaled = temp * lax.dot_general(rows, block, NT, preferred_element_type=F32)
        logits = scaled + bias
        small = jnp.exp(-jnp.abs(logits))
        inverse = 1.0 / (1.0 + small)
        grads = jnp.where(logits >= 0, inverse, small * inverse)
        mark = None
        if own and i == 0:
            shape = logits.shape
            mark = lax.broadcasted_iota(jnp.int32, shape, 0) == lax.broadcasted_iota(
                jnp.int32, shape, 1
            )
            grads = jnp.where(mark, grads - 1.0, grads)
        if stats:
            signed = logits if mark is None else jnp.where(mark, -logits, logits)
            terms = jnp.maximum(signed, 0.0) + jnp.log1p(small)
            width = logits.shape[1]
            three = [
                jnp.sum(v, axis=0, keepdims=True) for v in (terms, grads, grads * scaled)
            ]
            tile = jnp.concatenate([*three, jnp.zeros((5, width), F32)], axis=0)
            if width < ROWS:
                tile = jnp.concatenate([tile, jnp.zeros((8, ROWS - width), F32)], axis=1)
            sums = tile if sums is None else sums + tile
        part = jnp.dot(grads.astype(BF16), block, preferred_element_type=F32)
        total = part if total is None else total + part
    total_out[...] = total
    if stats:
        refs[0][...] = sums


def pairs(scale, emb, cols, state, own, stats, name):
    n = sum(c.shape[0] for group in cols for c in group)
    got = call(
        functools.partial(
            pair_kernel, len(emb), [len(g) for g in cols], own, stats, state is not None
        ),
        [scale, *emb, *(c for group in cols for c in group), *(state or ())],
        [out((ROWS, D), F32)] + ([out((8, ROWS), F32)] if stats else []),
        4 * ROWS * n * D,
        name,
    )
    return tuple(got)


def choose_kernel(place, *refs):
    chosen = refs[-1]

    @pl.when(place[3] == 1)
    def _():
        for i in range(CHUNKS):
            chosen[i * CH : (i + 1) * CH] = refs[i][...]

    @pl.when(place[3] == 0)
    def _():
        for i in range(CHUNKS):
            chosen[i * CH : (i + 1) * CH] = refs[CHUNKS + i][...]


def choose(place, near, far):
    return call(choose_kernel, [place, *near, *far], [out((ROWS, D), BF16)], 0, "choose")[0]


def order_kernel(feats, rows):
    values = feats[...]
    row = lax.broadcasted_iota(jnp.int32, (D, RW), 0)
    col = lax.broadcasted_iota(jnp.int32, (D, RW), 1)
    wanted = jnp.where(col < RC, col + lax.div(col, PC) * (3 * PC), -D)
    for c in range(2):
        for h in range(2):
            pick = (row == wanted + (c * PC + h * 2 * PC)).astype(F32).astype(BF16)
            rows[c * 2 + h] = jnp.dot(values, pick, preferred_element_type=F32).astype(BF16)


def ordered(feats):
    return call(
        order_kernel, [feats], [out((4, ROWS, RW), BF16)], 2 * ROWS * D * D, "ordered", scalars=0
    )[0]


def three_parts(value):
    high = value.astype(BF16).astype(F32)
    rest = value - high
    middle = rest.astype(BF16).astype(F32)
    lane = lax.broadcasted_iota(jnp.int32, (SV, RW), 1)
    parts = jnp.where(lane == 0, high, jnp.where(lane == 1, middle, jnp.where(lane == 2, rest - middle, 0.0)))
    return parts.astype(BF16)


def joined(rows):
    return jnp.sum(rows.astype(F32), axis=1, keepdims=True)


def tangent_kernel(scale, place, total, unit0, unit1, norm0, norm1, feats, sums, dz, message, scalars):
    core = place[0]
    lows = []
    for i, (unit, norm) in enumerate(((unit0, norm0), (unit1, norm1))):
        grad = scale[0] * total[i * CH : (i + 1) * CH]
        e = unit[...]
        along = jnp.sum(e * grad, axis=-1, keepdims=True)
        lows.append(((grad - e * along) * (1.0 / norm[...])).astype(BF16))
    low = jnp.concatenate(lows, axis=0)
    dz[...] = low
    for half in range(2):
        part = lax.dot_general(low, feats[(1 - core) * 2 + half], TN, preferred_element_type=F32)
        message[half * D : (half + 1) * D] = part.astype(BF16)
    value = jnp.sum(sums[...], axis=1, keepdims=True)
    value = jnp.concatenate([value, jnp.zeros((SV - 8, 1), F32)], axis=0)
    scalars[...] = value
    message[2 * D :] = three_parts(value)


def tangent(scale, place, total, unit, norm, feats, sums):
    return call(
        tangent_kernel,
        [scale, place, total, *unit, *norm, feats, sums],
        [out((ROWS, D), BF16), out((2 * D + SV, RW), BF16), out((SV, 1), F32)],
        2 * ROWS * D * D // 2,
        "tangent",
        scalars=2,
    )


def keep_kernel(place, dz, feats, kept):
    core = place[0]
    for half in range(2):
        kept[half * D : (half + 1) * D] = lax.dot_general(
            dz[...], feats[core * 2 + half], TN, preferred_element_type=F32
        )


def keep(place, dz, feats, name):
    return call(keep_kernel, [place, dz, feats], [out((2 * D, RW), F32)], ROWS * D * D, name)[0]


def back_kernel(dz, head, grad):
    grad[...] = lax.dot_general(dz[...], head[...], NT, preferred_element_type=F32).astype(BF16)


def back(dz, head):
    return call(
        back_kernel, [dz, head], [out((ROWS, D), BF16)], 2 * ROWS * D * D, "back", scalars=0
    )[0]


def first_kernel(place, kept, got, scalars, own, own_scalars, *messages):
    core, x, y = place[0], place[1], place[2]
    mine = jnp.where(core == 0, y, x)

    def block(t, u):
        number = jnp.where(core == 0, u * 4 + t, t * 4 + u)
        rows = pl.ds(pl.multiple_of(number * GC, GC), GC)
        return kept[rows] + got[rows].astype(F32)

    value = scalars[...] + joined(got[2 * D :])
    own_scalars[...] = value
    parts = three_parts(value)
    for by, message in enumerate(messages, 1):
        t = lax.rem(mine + by, 4)
        for u in range(4):
            message[u * GC : (u + 1) * GC] = block(t, u).astype(BF16)
        message[4 * GC :] = parts
    for u in range(4):
        own[u * GC : (u + 1) * GC] = block(mine, u)


def second_kernel(place, own, scalars, one, two, three, mine, own_scalars, *messages):
    core, x, y = place[0], place[1], place[2]
    other = jnp.where(core == 0, x, y)

    def block(u):
        rows = pl.ds(pl.multiple_of(u * GC, GC), GC)
        return (own[rows] + one[rows].astype(F32)) + (
            two[rows].astype(F32) + three[rows].astype(F32)
        )

    value = scalars[...]
    for ref in (one, two, three):
        value = value + joined(ref[4 * GC :])
    own_scalars[...] = value
    parts = three_parts(value)
    for by, message in enumerate(messages, 1):
        message[:GC] = block(lax.rem(other + by, 4)).astype(BF16)
        message[GC:] = parts
    mine[...] = block(other)


def third_kernel(own, scalars, one, two, three, turned, own_scalars):
    total = (own[...] + one[:GC].astype(F32)) + (
        two[:GC].astype(F32) + three[:GC].astype(F32)
    )
    value = scalars[...]
    for ref in (one, two, three):
        value = value + joined(ref[GC:])
    own_scalars[...] = value
    turned[...] = total.T[:RC]


def pieces_kernel(img, scalars, own, one, two, three, pieces):
    total = (own[...] + one[:GC].astype(F32)) + (
        two[:GC].astype(F32) + three[:GC].astype(F32)
    )
    tail = three_parts(scalars[...])[: TAIL, :GC]
    for i in range(8):
        rows = slice(i * PC, (i + 1) * PC)
        both = jnp.concatenate([img[rows], total.T[rows], tail.astype(F32)], axis=0)
        pieces[i] = both.astype(BF16)


def last_kernel(got, img, txt, scalars):
    total = got[0].astype(F32)
    for i in range(1, 8):
        total = total + got[i].astype(F32)
    img[...] = total[:PC]
    txt[...] = total[PC : 2 * PC]
    scalars[...] = jnp.sum(total[2 * PC :], axis=1, keepdims=True) / COUNT


def first(place, kept, got, scalars):
    own, scalars, *messages = call(
        first_kernel,
        [place, kept, got, scalars],
        [out((4 * GC, RW), F32), out((SV, 1), F32)] + [out((4 * GC + SV, RW), BF16)] * 3,
        0,
        "first",
    )
    return own, scalars, [send(m, first_axis(by)) for by, m in enumerate(messages, 1)]


def second(place, own, scalars, got):
    own, scalars, *messages = call(
        second_kernel,
        [place, own, scalars, *got],
        [out((GC, RW), F32), out((SV, 1), F32)] + [out((GC + SV, RW), BF16)] * 3,
        0,
        "second",
    )
    return own, scalars, [send(m, second_axis(by)) for by, m in enumerate(messages, 1)]


def third(own, scalars, got):
    return call(
        third_kernel,
        [own, scalars, *got],
        [out((RC, GC), F32), out((SV, 1), F32)],
        0,
        "third",
        scalars=0,
    )


def across_z(img, scalars, own, got):
    (pieces,) = call(
        pieces_kernel,
        [img, scalars, own, *got],
        [out((8, 2 * PC + TAIL, GC), BF16)],
        0,
        "pieces",
        scalars=0,
    )
    return call(
        last_kernel,
        [lax.all_to_all(pieces, "z", 0, 0)],
        [out((PC, GC), F32), out((PC, GC), F32), out((TAIL, 1), F32)],
        0,
        "last",
        scalars=0,
    )


def after(done, *values):
    got = lax.optimization_barrier((*values, done))[: len(values)]
    return got[0] if len(values) == 1 else got


def local(img_feats, txt_feats, img_head, txt_head, log_temp, bias):
    core, xh = lax.axis_index("core"), lax.axis_index("xh")
    x = xh * 2 + lax.axis_index("xl")
    place = jnp.stack([core, x, lax.axis_index("y"), xh == core]).astype(jnp.int32)
    scale = jnp.stack([jnp.exp(log_temp), bias])

    feats = after((place, scale), txt_feats)
    t0, txt_unit0, txt_norm0 = embed(feats, txt_head, 0, "embed_t0")
    near_t0 = send(t0, to_partner)
    t1, txt_unit1, txt_norm1, txt = embed(feats, txt_head, CH, "embed_t1", [t0])
    near_t1, sib_t = send(t1, to_partner), send(txt, to_sibling)
    feats = after(t1, img_feats)
    i0, img_unit0, img_norm0 = embed(feats, img_head, 0, "embed_i0")
    near_i0 = send(i0, to_partner)
    i1, img_unit1, img_norm1, img = embed(feats, img_head, CH, "embed_i1", [i0])
    near_i1, sib_i = send(i1, to_partner), send(img, to_sibling)
    txt_unit, txt_norm = [txt_unit0, txt_unit1], [txt_norm0, txt_norm1]
    img_unit, img_norm = [img_unit0, img_unit1], [img_norm0, img_norm1]

    img_rows = ordered(after(img, img_feats))
    txt_rows = ordered(after(img_rows, txt_feats))
    near_t0 = after(txt_rows, near_t0)
    far_t0 = send(near_t0, onward)
    a = pairs(scale, [img], [[near_t0]], None, False, True, "near_a0")
    a = pairs(scale, [img], [[txt], [sib_t]], a, True, True, "own_a")
    (b,) = pairs(after(a[1], scale), [txt], [[img], [sib_i]], None, True, False, "own_b")
    near_t1 = after(b, near_t1)
    far_t1 = send(near_t1, onward)
    a = pairs(scale, [img], [[near_t1, far_t0]], a, False, True, "near_a1")
    chosen_t = choose(after(a[1], place), [near_t0, near_t1], [far_t0, far_t1])
    last_t = send(chosen_t, to_sibling)
    near_i0 = after(a[1], near_i0)
    far_i0 = send(near_i0, onward)
    (b,) = pairs(after(chosen_t, scale), [txt], [[near_i0]], (b,), False, False, "near_b0")
    a = pairs(after(b, scale), [img], [[far_t1]], a, False, True, "far_a")
    a = pairs(scale, [img], [[last_t]], a, False, True, "last_a")
    dz_img, message, scalars = tangent(scale, place, a[0], img_unit, img_norm, img_rows, a[1])
    got = send(message, to_sibling)
    near_i1 = after(dz_img, near_i1)
    far_i1 = send(near_i1, onward)
    (b,) = pairs(scale, [txt], [[near_i1, far_i0]], (b,), False, False, "near_b1")
    kept = keep(after(b, place), dz_img, img_rows, "keep_img")
    own, scalars, got = first(place, kept, got, scalars)
    grad_img_feats = back(after(own, dz_img), img_head)
    chosen_i = choose(after(grad_img_feats, place), [near_i0, near_i1], [far_i0, far_i1])
    last_i = send(chosen_i, to_sibling)
    (b,) = pairs(after(chosen_i, scale), [txt], [[far_i1]], (b,), False, False, "far_b")
    (b,) = pairs(scale, [txt], [[last_i]], (b,), False, False, "last_b")
    none = jnp.zeros((8, ROWS), F32)
    dz_txt, message, no_scalars = tangent(scale, place, b, txt_unit, txt_norm, txt_rows, none)
    got_txt = send(message, to_sibling)
    kept = keep(place, dz_txt, txt_rows, "keep_txt")
    own, scalars, got = second(after(kept, place), own, scalars, got)
    own_txt, no_scalars, got_txt = first(after(own, place), kept, got_txt, no_scalars)
    img_turned, scalars = third(after(own_txt, own), scalars, got)
    grad_txt_feats = back(after(img_turned, dz_txt), txt_head)
    own, no_scalars, got = second(after(grad_txt_feats, place), own_txt, no_scalars, got_txt)
    grad_img_head, grad_txt_head, scalars = across_z(img_turned, scalars, own, got)
    loss, grad_bias, grad_log_temp = (scalars[i, 0] for i in range(3))
    return (
        loss,
        grad_log_temp,
        grad_bias,
        grad_img_feats,
        grad_txt_feats,
        grad_img_head,
        grad_txt_head,
    )


def solution(mesh):
    fine = Mesh(mesh.devices.reshape(SIZES), AXES)
    rows = P(AXES, None)
    tile = P(AXES[:3], AXES[3:])
    return jax.shard_map(
        local,
        mesh=fine,
        in_specs=(rows, rows, P(), P(), P(), P()),
        out_specs=(P(), P(), P(), rows, rows, tile, tile),
        check_vma=False,
    )
```

```python
import functools

import jax
import jax.numpy as jnp
import numpy as np
from jax import lax
from jax.experimental import pallas as pl
from jax.experimental.pallas import tpu as pltpu
from jax.sharding import Mesh
from jax.sharding import PartitionSpec as P

AXES = ("z", "xh", "core", "xl", "y")
SIZES = (8, 2, 2, 2, 4)
ROUNDS = 2
TAIL = 4
ROWS = 448
D = 1152
CHUNKS = 2
CH = ROWS // CHUNKS
GC = 144
RC = 288
RW = 384
PC = 36
SV = 16
COUNT = 256 * ROWS * ROWS * (2 * ROUNDS + 1)
COST = {"own_a": 30, "own_b": 30, "keep_img": 30, "near_b0": 30, "second": 16}
F32 = jnp.float32
BF16 = jnp.bfloat16
NT = (((1,), (1,)), ((), ()))
TN = (((0,), (0,)), ((), ()))


def permutation(move):
    pairs = []
    for source in range(int(np.prod(SIZES))):
        z, xh, core, xl, y = (int(i) for i in np.unravel_index(source, SIZES))
        place = {"z": z, "x": xh * 2 + xl, "y": y, "core": core}
        place = {**place, **move(place)}
        x = place["x"] % 4
        target = (place["z"] % 8, x // 2, place["core"] % 2, x % 2, place["y"] % 4)
        pairs.append((source, int(np.ravel_multi_index(target, SIZES))))
    return pairs


def send(value, move):
    return lax.ppermute(value, AXES, permutation(move))


def to_partner(p):
    return {"x": p["x"] + 2}


def onward(p):
    return {"z": p["z"] + (1 if p["x"] < 2 else -1)}


def to_sibling(p):
    return {"core": p["core"] + 1}


def first_axis(by):
    return lambda p: {"y": p["y"] + by} if p["core"] == 0 else {"x": p["x"] + by}


def second_axis(by):
    return lambda p: {"x": p["x"] + by} if p["core"] == 0 else {"y": p["y"] + by}


VMEM = pl.BlockSpec(memory_space=pltpu.VMEM)
SMEM = pl.BlockSpec(memory_space=pltpu.SMEM)


def call(kernel, inputs, outputs, flops, name, scalars=1, limit=24):
    size = sum(int(np.prod(a.shape)) * a.dtype.itemsize for a in [*inputs, *outputs])
    return pl.pallas_call(
        kernel,
        out_shape=tuple(outputs),
        in_specs=[SMEM] * scalars + [VMEM] * (len(inputs) - scalars),
        out_specs=tuple(VMEM for _ in outputs),
        compiler_params=pltpu.CompilerParams(vmem_limit_bytes=limit * 1024 * 1024),
        cost_estimate=pl.CostEstimate(flops=COST.get(name, 0) * 10**9, bytes_accessed=0, transcendentals=0),
        name=name,
    )(*inputs)


def out(shape, dtype):
    return jax.ShapeDtypeStruct(shape, dtype)


def embed_kernel(start, feats, head, *refs):
    z = jnp.dot(feats[start : start + CH], head[...], preferred_element_type=F32)
    n = jnp.sqrt(jnp.sum(z * z, axis=-1, keepdims=True) + 1e-06)
    e = z * (1.0 / n)
    low = e.astype(BF16)
    emb, unit, norm = refs[-3:] if start == 0 else refs[1:4]
    unit[...] = e
    norm[...] = n
    emb[...] = low
    if start:
        refs[4][:start] = refs[0][...]
        refs[4][start:] = low


def embed(feats, head, start, name, earlier=()):
    shapes = [out((CH, D), BF16), out((CH, D), F32), out((CH, 1), F32)]
    return call(
        functools.partial(embed_kernel, start),
        [feats, head, *earlier],
        shapes + [out((ROWS, D), BF16)] * len(earlier),
        2 * CH * D * D,
        name,
        scalars=0,
    )


def whole(refs):
    values = [r[...] for r in refs]
    return values[0] if len(values) == 1 else jnp.concatenate(values, axis=0)


def pair_kernel(rows_in, blocks, own, stats, more, *refs):
    refs = list(refs)
    scale = refs.pop(0)
    rows = whole([refs.pop(0) for _ in range(rows_in)])
    cols = [[refs.pop(0) for _ in range(n)] for n in blocks]
    before = [refs.pop(0) for _ in range((2 if stats else 1) if more else 0)]
    total_out = refs.pop(0)
    temp, bias = scale[0], scale[1]
    total = before[0][...] if more else None
    sums = before[1][...] if more and stats else None
    for i, group in enumerate(cols):
        block = whole(group)
        scaled = temp * lax.dot_general(rows, block, NT, preferred_element_type=F32)
        logits = scaled + bias
        small = jnp.exp(-jnp.abs(logits))
        inverse = 1.0 / (1.0 + small)
        grads = jnp.where(logits >= 0, inverse, small * inverse)
        mark = None
        if own and i == 0:
            shape = logits.shape
            mark = lax.broadcasted_iota(jnp.int32, shape, 0) == lax.broadcasted_iota(
                jnp.int32, shape, 1
            )
            grads = jnp.where(mark, grads - 1.0, grads)
        if stats:
            signed = logits if mark is None else jnp.where(mark, -logits, logits)
            terms = jnp.maximum(signed, 0.0) + jnp.log1p(small)
            width = logits.shape[1]
            three = [
                jnp.sum(v, axis=0, keepdims=True) for v in (terms, grads, grads * scaled)
            ]
            tile = jnp.concatenate([*three, jnp.zeros((5, width), F32)], axis=0)
            if width < ROWS:
                tile = jnp.concatenate([tile, jnp.zeros((8, ROWS - width), F32)], axis=1)
            sums = tile if sums is None else sums + tile
        part = jnp.dot(grads.astype(BF16), block, preferred_element_type=F32)
        total = part if total is None else total + part
    total_out[...] = total
    if stats:
        refs[0][...] = sums


def pairs(scale, emb, cols, state, own, stats, name):
    n = sum(c.shape[0] for group in cols for c in group)
    got = call(
        functools.partial(
            pair_kernel, len(emb), [len(g) for g in cols], own, stats, state is not None
        ),
        [scale, *emb, *(c for group in cols for c in group), *(state or ())],
        [out((ROWS, D), F32)] + ([out((8, ROWS), F32)] if stats else []),
        4 * ROWS * n * D,
        name,
    )
    return tuple(got)


def choose_kernel(place, *refs):
    chosen = refs[-1]

    @pl.when(place[3] == 1)
    def _():
        for i in range(CHUNKS):
            chosen[i * CH : (i + 1) * CH] = refs[i][...]

    @pl.when(place[3] == 0)
    def _():
        for i in range(CHUNKS):
            chosen[i * CH : (i + 1) * CH] = refs[CHUNKS + i][...]


def choose(place, near, far):
    return call(choose_kernel, [place, *near, *far], [out((ROWS, D), BF16)], 0, "choose")[0]


def order_kernel(feats, rows):
    values = feats[...]
    row = lax.broadcasted_iota(jnp.int32, (D, RW), 0)
    col = lax.broadcasted_iota(jnp.int32, (D, RW), 1)
    wanted = jnp.where(col < RC, col + lax.div(col, PC) * (3 * PC), -D)
    for c in range(2):
        for h in range(2):
            pick = (row == wanted + (c * PC + h * 2 * PC)).astype(F32).astype(BF16)
            rows[c * 2 + h] = jnp.dot(values, pick, preferred_element_type=F32).astype(BF16)


def ordered(feats):
    return call(
        order_kernel, [feats], [out((4, ROWS, RW), BF16)], 2 * ROWS * D * D, "ordered", scalars=0
    )[0]


def three_parts(value):
    high = value.astype(BF16).astype(F32)
    rest = value - high
    middle = rest.astype(BF16).astype(F32)
    lane = lax.broadcasted_iota(jnp.int32, (SV, RW), 1)
    parts = jnp.where(lane == 0, high, jnp.where(lane == 1, middle, jnp.where(lane == 2, rest - middle, 0.0)))
    return parts.astype(BF16)


def joined(rows):
    return jnp.sum(rows.astype(F32), axis=1, keepdims=True)


def tangent_kernel(scale, place, total, unit0, unit1, norm0, norm1, feats, sums, dz, message, scalars):
    core = place[0]
    lows = []
    for i, (unit, norm) in enumerate(((unit0, norm0), (unit1, norm1))):
        grad = scale[0] * total[i * CH : (i + 1) * CH]
        e = unit[...]
        along = jnp.sum(e * grad, axis=-1, keepdims=True)
        lows.append(((grad - e * along) * (1.0 / norm[...])).astype(BF16))
    low = jnp.concatenate(lows, axis=0)
    dz[...] = low
    for half in range(2):
        part = lax.dot_general(low, feats[(1 - core) * 2 + half], TN, preferred_element_type=F32)
        message[half * D : (half + 1) * D] = part.astype(BF16)
    value = jnp.sum(sums[...], axis=1, keepdims=True)
    value = jnp.concatenate([value, jnp.zeros((SV - 8, 1), F32)], axis=0)
    scalars[...] = value
    message[2 * D :] = three_parts(value)


def tangent(scale, place, total, unit, norm, feats, sums):
    return call(
        tangent_kernel,
        [scale, place, total, *unit, *norm, feats, sums],
        [out((ROWS, D), BF16), out((2 * D + SV, RW), BF16), out((SV, 1), F32)],
        2 * ROWS * D * D // 2,
        "tangent",
        scalars=2,
    )


def keep_kernel(place, dz, feats, kept):
    core = place[0]
    for half in range(2):
        kept[half * D : (half + 1) * D] = lax.dot_general(
            dz[...], feats[core * 2 + half], TN, preferred_element_type=F32
        )


def keep(place, dz, feats, name):
    return call(keep_kernel, [place, dz, feats], [out((2 * D, RW), F32)], ROWS * D * D, name)[0]


def back_kernel(dz, head, grad):
    grad[...] = lax.dot_general(dz[...], head[...], NT, preferred_element_type=F32).astype(BF16)


def back(dz, head, name):
    return call(
        back_kernel, [dz, head], [out((ROWS, D), BF16)], 2 * ROWS * D * D, name, scalars=0
    )[0]


def first_kernel(place, kept, got, scalars, own, own_scalars, *messages):
    core, x, y = place[0], place[1], place[2]
    mine = jnp.where(core == 0, y, x)

    def block(t, u):
        number = jnp.where(core == 0, u * 4 + t, t * 4 + u)
        rows = pl.ds(pl.multiple_of(number * GC, GC), GC)
        return kept[rows] + got[rows].astype(F32)

    value = scalars[...] + joined(got[2 * D :])
    own_scalars[...] = value
    parts = three_parts(value)
    for by, message in enumerate(messages, 1):
        t = lax.rem(mine + by, 4)
        for u in range(4):
            message[u * GC : (u + 1) * GC] = block(t, u).astype(BF16)
        message[4 * GC :] = parts
    for u in range(4):
        own[u * GC : (u + 1) * GC] = block(mine, u)


def second_kernel(place, own, scalars, one, two, three, mine, own_scalars, *messages):
    core, x, y = place[0], place[1], place[2]
    other = jnp.where(core == 0, x, y)

    def block(u):
        rows = pl.ds(pl.multiple_of(u * GC, GC), GC)
        return (own[rows] + one[rows].astype(F32)) + (
            two[rows].astype(F32) + three[rows].astype(F32)
        )

    value = scalars[...]
    for ref in (one, two, three):
        value = value + joined(ref[4 * GC :])
    own_scalars[...] = value
    parts = three_parts(value)
    for by, message in enumerate(messages, 1):
        message[:GC] = block(lax.rem(other + by, 4)).astype(BF16)
        message[GC:] = parts
    mine[...] = block(other)


def third_kernel(own, scalars, one, two, three, turned, own_scalars):
    total = (own[...] + one[:GC].astype(F32)) + (
        two[:GC].astype(F32) + three[:GC].astype(F32)
    )
    value = scalars[...]
    for ref in (one, two, three):
        value = value + joined(ref[GC:])
    own_scalars[...] = value
    turned[...] = total.T[:RC]


def pieces_kernel(img, scalars, own, one, two, three, pieces):
    total = (own[...] + one[:GC].astype(F32)) + (
        two[:GC].astype(F32) + three[:GC].astype(F32)
    )
    both = jnp.concatenate([img[...], total.T[:RC]], axis=1)
    tail = three_parts(scalars[...])[:TAIL, : 2 * GC].astype(F32)
    for i in range(8):
        rows = both[i * PC : (i + 1) * PC]
        pieces[i] = jnp.concatenate([rows, tail], axis=0).astype(BF16)


def last_kernel(got, img, txt, scalars):
    total = got[0].astype(F32)
    for i in range(1, 8):
        total = total + got[i].astype(F32)
    img[...] = total[:PC, :GC]
    txt[...] = total[:PC, GC:]
    scalars[...] = jnp.sum(total[PC:], axis=1, keepdims=True) / COUNT


def first(place, kept, got, scalars):
    own, scalars, *messages = call(
        first_kernel,
        [place, kept, got, scalars],
        [out((4 * GC, RW), F32), out((SV, 1), F32)] + [out((4 * GC + SV, RW), BF16)] * 3,
        0,
        "first",
    )
    return own, scalars, [send(m, first_axis(by)) for by, m in enumerate(messages, 1)]


def second(place, own, scalars, got):
    own, scalars, *messages = call(
        second_kernel,
        [place, own, scalars, *got],
        [out((GC, RW), F32), out((SV, 1), F32)] + [out((GC + SV, RW), BF16)] * 3,
        0,
        "second",
    )
    return own, scalars, [send(m, second_axis(by)) for by, m in enumerate(messages, 1)]


def third(own, scalars, got):
    return call(
        third_kernel,
        [own, scalars, *got],
        [out((RC, GC), F32), out((SV, 1), F32)],
        0,
        "third",
        scalars=0,
    )


def across_z(img, scalars, own, got):
    (pieces,) = call(
        pieces_kernel,
        [img, scalars, own, *got],
        [out((8, PC + TAIL, 2 * GC), BF16)],
        0,
        "pieces",
        scalars=0,
    )
    return call(
        last_kernel,
        [lax.all_to_all(pieces, "z", 0, 0)],
        [out((PC, GC), F32), out((PC, GC), F32), out((TAIL, 1), F32)],
        0,
        "last",
        scalars=0,
    )


def after(done, *values):
    got = lax.optimization_barrier((*values, done))[: len(values)]
    return got[0] if len(values) == 1 else got


def local(img_feats, txt_feats, img_head, txt_head, log_temp, bias):
    core, xh = lax.axis_index("core"), lax.axis_index("xh")
    x = xh * 2 + lax.axis_index("xl")
    place = jnp.stack([core, x, lax.axis_index("y"), xh == core]).astype(jnp.int32)
    scale = jnp.stack([jnp.exp(log_temp), bias])

    feats = after((place, scale), txt_feats)
    t0, txt_unit0, txt_norm0 = embed(feats, txt_head, 0, "embed_t0")
    near_t0 = send(t0, to_partner)
    t1, txt_unit1, txt_norm1, txt = embed(feats, txt_head, CH, "embed_t1", [t0])
    near_t1, sib_t = send(t1, to_partner), send(txt, to_sibling)
    feats = after(t1, img_feats)
    i0, img_unit0, img_norm0 = embed(feats, img_head, 0, "embed_i0")
    near_i0 = send(i0, to_partner)
    i1, img_unit1, img_norm1, img = embed(feats, img_head, CH, "embed_i1", [i0])
    near_i1, sib_i = send(i1, to_partner), send(img, to_sibling)
    txt_unit, txt_norm = [txt_unit0, txt_unit1], [txt_norm0, txt_norm1]
    img_unit, img_norm = [img_unit0, img_unit1], [img_norm0, img_norm1]

    img_rows = ordered(after(img, img_feats))
    txt_rows = ordered(after(img_rows, txt_feats))
    near_t0 = after(txt_rows, near_t0)
    far_t0 = send(near_t0, onward)
    a = pairs(scale, [img], [[near_t0]], None, False, True, "near_a0")
    a = pairs(scale, [img], [[txt], [sib_t]], a, True, True, "own_a")
    (b,) = pairs(after(a[1], scale), [txt], [[img], [sib_i]], None, True, False, "own_b")
    near_t1 = after(b, near_t1)
    far_t1 = send(near_t1, onward)
    a = pairs(scale, [img], [[near_t1, far_t0]], a, False, True, "near_a1")
    chosen_t = choose(after(a[1], place), [near_t0, near_t1], [far_t0, far_t1])
    last_t = send(chosen_t, to_sibling)
    near_i0 = after(a[1], near_i0)
    far_i0 = send(near_i0, onward)
    (b,) = pairs(after(chosen_t, scale), [txt], [[near_i0]], (b,), False, False, "near_b0")
    a = pairs(after(b, scale), [img], [[far_t1]], a, False, True, "far_a")
    near_i1 = after(a[1], near_i1)
    far_i1 = send(near_i1, onward)
    (b,) = pairs(after(a[1], scale), [txt], [[near_i1, far_i0]], (b,), False, False, "near_b1")
    a = pairs(after(b, scale), [img], [[last_t]], a, False, True, "last_a")
    dz_img, message, scalars = tangent(scale, place, a[0], img_unit, img_norm, img_rows, a[1])
    got = send(message, to_sibling)
    kept = keep(place, dz_img, img_rows, "keep_img")
    chosen_i = choose(after(kept, place), [near_i0, near_i1], [far_i0, far_i1])
    last_i = send(chosen_i, to_sibling)
    own, scalars, got = first(after(chosen_i, place), kept, got, scalars)
    (b,) = pairs(after(own, scale), [txt], [[far_i1]], (b,), False, False, "far_b")
    (b,) = pairs(scale, [txt], [[last_i]], (b,), False, False, "last_b")
    none = jnp.zeros((8, ROWS), F32)
    dz_txt, message, no_scalars = tangent(scale, place, b, txt_unit, txt_norm, txt_rows, none)
    got_txt = send(message, to_sibling)
    kept = keep(place, dz_txt, txt_rows, "keep_txt")
    own, scalars, got = second(after(kept, place), own, scalars, got)
    own_txt, no_scalars, got_txt = first(after(own, place), kept, got_txt, no_scalars)
    grad_txt_feats = back(after(own_txt, dz_txt), txt_head, "back_txt")
    own_x, no_scalars, got_x = second(after(grad_txt_feats, place), own_txt, no_scalars, got_txt)
    img_turned, scalars = third(after(own_x, own), scalars, got)
    grad_img_feats = back(after(img_turned, dz_img), img_head, "back_img")
    own, got = after(grad_img_feats, own_x), got_x
    grad_img_head, grad_txt_head, scalars = across_z(img_turned, scalars, own, got)
    loss, grad_bias, grad_log_temp = (scalars[i, 0] for i in range(3))
    return (
        loss,
        grad_log_temp,
        grad_bias,
        grad_img_feats,
        grad_txt_feats,
        grad_img_head,
        grad_txt_head,
    )


def solution(mesh):
    fine = Mesh(mesh.devices.reshape(SIZES), AXES)
    rows = P(AXES, None)
    tile = P(AXES[:3], AXES[3:])
    return jax.shard_map(
        local,
        mesh=fine,
        in_specs=(rows, rows, P(), P(), P(), P()),
        out_specs=(P(), P(), P(), rows, rows, tile, tile),
        check_vma=False,
    )
```

```python
import functools

import jax
import jax.numpy as jnp
import numpy as np
from jax import lax
from jax.experimental import pallas as pl
from jax.experimental.pallas import tpu as pltpu
from jax.sharding import Mesh
from jax.sharding import PartitionSpec as P

AXES = ("z", "xh", "core", "xl", "y")
SIZES = (8, 2, 2, 2, 4)
ROUNDS = 2
TAIL = 4
ROWS = 448
D = 1152
CHUNKS = 2
CH = ROWS // CHUNKS
GC = 144
RC = 288
SPARE = 96
RW = 384
PC = 36
SV = 16
COUNT = 256 * ROWS * ROWS * (2 * ROUNDS + 1)
COST = {"own_a": 30, "own_b": 30, "near_b0": 30, "keep_img": 30, "keep_txt": 16}
F32 = jnp.float32
BF16 = jnp.bfloat16
NT = (((1,), (1,)), ((), ()))
TN = (((0,), (0,)), ((), ()))


def permutation(move):
    pairs = []
    for source in range(int(np.prod(SIZES))):
        z, xh, core, xl, y = (int(i) for i in np.unravel_index(source, SIZES))
        place = {"z": z, "x": xh * 2 + xl, "y": y, "core": core}
        place = {**place, **move(place)}
        x = place["x"] % 4
        target = (place["z"] % 8, x // 2, place["core"] % 2, x % 2, place["y"] % 4)
        pairs.append((source, int(np.ravel_multi_index(target, SIZES))))
    return pairs


def send(value, move):
    return lax.ppermute(value, AXES, permutation(move))


def to_partner(p):
    return {"x": p["x"] + 2}


def onward(p):
    return {"z": p["z"] + (1 if p["x"] < 2 else -1)}


def to_sibling(p):
    return {"core": p["core"] + 1}


def first_axis(by):
    return lambda p: {"y": p["y"] + by} if p["core"] == 0 else {"x": p["x"] + by}


def second_axis(by):
    return lambda p: {"x": p["x"] + by} if p["core"] == 0 else {"y": p["y"] + by}


VMEM = pl.BlockSpec(memory_space=pltpu.VMEM)
SMEM = pl.BlockSpec(memory_space=pltpu.SMEM)


def call(kernel, inputs, outputs, flops, name, scalars=1, limit=24, scratch=()):
    size = sum(int(np.prod(a.shape)) * a.dtype.itemsize for a in [*inputs, *outputs])
    return pl.pallas_call(
        kernel,
        out_shape=tuple(outputs),
        in_specs=[SMEM] * scalars + [VMEM] * (len(inputs) - scalars),
        out_specs=tuple(VMEM for _ in outputs),
        scratch_shapes=scratch,
        compiler_params=pltpu.CompilerParams(vmem_limit_bytes=limit * 1024 * 1024),
        cost_estimate=pl.CostEstimate(flops=COST.get(name, 0) * 10**9, bytes_accessed=0, transcendentals=0),
        name=name,
    )(*inputs)


def out(shape, dtype):
    return jax.ShapeDtypeStruct(shape, dtype)


def embed_kernel(start, feats, head, *refs):
    z = jnp.dot(feats[start : start + CH], head[...], preferred_element_type=F32)
    n = jnp.sqrt(jnp.sum(z * z, axis=-1, keepdims=True) + 1e-06)
    e = z * (1.0 / n)
    low = e.astype(BF16)
    emb, unit, norm = refs[-3:] if start == 0 else refs[1:4]
    unit[...] = e
    norm[...] = n
    emb[...] = low
    if start:
        refs[4][:start] = refs[0][...]
        refs[4][start:] = low


def embed(feats, head, start, name, earlier=()):
    shapes = [out((CH, D), BF16), out((CH, D), F32), out((CH, 1), F32)]
    return call(
        functools.partial(embed_kernel, start),
        [feats, head, *earlier],
        shapes + [out((ROWS, D), BF16)] * len(earlier),
        2 * CH * D * D,
        name,
        scalars=0,
    )


def whole(refs):
    values = [r[...] for r in refs]
    return values[0] if len(values) == 1 else jnp.concatenate(values, axis=0)


def pair_kernel(rows_in, blocks, own, stats, more, *refs):
    refs = list(refs)
    scale = refs.pop(0)
    rows = whole([refs.pop(0) for _ in range(rows_in)])
    cols = [[refs.pop(0) for _ in range(n)] for n in blocks]
    before = [refs.pop(0) for _ in range((2 if stats else 1) if more else 0)]
    total_out = refs.pop(0)
    temp, bias = scale[0], scale[1]
    total = before[0][...] if more else None
    sums = before[1][...] if more and stats else None
    for i, group in enumerate(cols):
        block = whole(group)
        scaled = temp * lax.dot_general(rows, block, NT, preferred_element_type=F32)
        logits = scaled + bias
        small = jnp.exp(-jnp.abs(logits))
        inverse = 1.0 / (1.0 + small)
        grads = jnp.where(logits >= 0, inverse, small * inverse)
        mark = None
        if own and i == 0:
            shape = logits.shape
            mark = lax.broadcasted_iota(jnp.int32, shape, 0) == lax.broadcasted_iota(
                jnp.int32, shape, 1
            )
            grads = jnp.where(mark, grads - 1.0, grads)
        if stats:
            signed = logits if mark is None else jnp.where(mark, -logits, logits)
            terms = jnp.maximum(signed, 0.0) + jnp.log1p(small)
            width = logits.shape[1]
            three = [
                jnp.sum(v, axis=0, keepdims=True) for v in (terms, grads, grads * scaled)
            ]
            tile = jnp.concatenate([*three, jnp.zeros((5, width), F32)], axis=0)
            if width < ROWS:
                tile = jnp.concatenate([tile, jnp.zeros((8, ROWS - width), F32)], axis=1)
            sums = tile if sums is None else sums + tile
        part = jnp.dot(grads.astype(BF16), block, preferred_element_type=F32)
        total = part if total is None else total + part
    total_out[...] = total
    if stats:
        refs[0][...] = sums


def pairs(scale, emb, cols, state, own, stats, name):
    n = sum(c.shape[0] for group in cols for c in group)
    got = call(
        functools.partial(
            pair_kernel, len(emb), [len(g) for g in cols], own, stats, state is not None
        ),
        [scale, *emb, *(c for group in cols for c in group), *(state or ())],
        [out((ROWS, D), F32)] + ([out((8, ROWS), F32)] if stats else []),
        4 * ROWS * n * D,
        name,
    )
    return tuple(got)


def choose_kernel(place, *refs):
    chosen = refs[-1]

    @pl.when(place[3] == 1)
    def _():
        for i in range(CHUNKS):
            chosen[i * CH : (i + 1) * CH] = refs[i][...]

    @pl.when(place[3] == 0)
    def _():
        for i in range(CHUNKS):
            chosen[i * CH : (i + 1) * CH] = refs[CHUNKS + i][...]


def choose(place, near, far):
    return call(choose_kernel, [place, *near, *far], [out((ROWS, D), BF16)], 0, "choose")[0]


def order_kernel(feats, rows):
    values = feats[...]
    row = lax.broadcasted_iota(jnp.int32, (D, RW), 0)
    col = lax.broadcasted_iota(jnp.int32, (D, RW), 1)
    wanted = jnp.where(col < RC, col + lax.div(col, PC) * (3 * PC), -D)
    for c in range(2):
        for h in range(2):
            pick = (row == wanted + (c * PC + h * 2 * PC)).astype(F32).astype(BF16)
            rows[c * 2 + h] = jnp.dot(values, pick, preferred_element_type=F32).astype(BF16)


def ordered(feats):
    return call(
        order_kernel, [feats], [out((4, ROWS, RW), BF16)], 2 * ROWS * D * D, "ordered", scalars=0
    )[0]


def three_parts(value):
    high = value.astype(BF16).astype(F32)
    rest = value - high
    middle = rest.astype(BF16).astype(F32)
    lane = lax.broadcasted_iota(jnp.int32, (SV, RW), 1)
    parts = jnp.where(lane == 0, high, jnp.where(lane == 1, middle, jnp.where(lane == 2, rest - middle, 0.0)))
    return parts.astype(BF16)


def joined(rows):
    return jnp.sum(rows.astype(F32), axis=1, keepdims=True)


def tangent_kernel(scale, place, total, unit0, unit1, norm0, norm1, feats, sums, dz, message, scalars):
    core = place[0]
    lows = []
    for i, (unit, norm) in enumerate(((unit0, norm0), (unit1, norm1))):
        grad = scale[0] * total[i * CH : (i + 1) * CH]
        e = unit[...]
        along = jnp.sum(e * grad, axis=-1, keepdims=True)
        lows.append(((grad - e * along) * (1.0 / norm[...])).astype(BF16))
    low = jnp.concatenate(lows, axis=0)
    dz[...] = low
    for half in range(2):
        part = lax.dot_general(low, feats[(1 - core) * 2 + half], TN, preferred_element_type=F32)
        message[half * D : (half + 1) * D] = part.astype(BF16)
    value = jnp.sum(sums[...], axis=1, keepdims=True)
    value = jnp.concatenate([value, jnp.zeros((SV - 8, 1), F32)], axis=0)
    scalars[...] = value
    message[2 * D :] = three_parts(value)


def tangent(scale, place, total, unit, norm, feats, sums):
    return call(
        tangent_kernel,
        [scale, place, total, *unit, *norm, feats, sums],
        [out((ROWS, D), BF16), out((2 * D + SV, RW), BF16), out((SV, 1), F32)],
        2 * ROWS * D * D // 2,
        "tangent",
        scalars=2,
    )


def keep_kernel(place, dz, feats, kept):
    core = place[0]
    for half in range(2):
        kept[half * D : (half + 1) * D] = lax.dot_general(
            dz[...], feats[core * 2 + half], TN, preferred_element_type=F32
        )


def keep(place, dz, feats, name):
    return call(keep_kernel, [place, dz, feats], [out((2 * D, RW), F32)], ROWS * D * D, name)[0]


def back_kernel(dz, head, grad):
    grad[...] = lax.dot_general(dz[...], head[...], NT, preferred_element_type=F32).astype(BF16)


def back(dz, head, name):
    return call(
        back_kernel, [dz, head], [out((ROWS, D), BF16)], 2 * ROWS * D * D, name, scalars=0
    )[0]


def first_kernel(place, kept, got, scalars, own, own_scalars, *messages):
    core, x, y = place[0], place[1], place[2]
    mine = jnp.where(core == 0, y, x)

    def block(t, u):
        number = jnp.where(core == 0, u * 4 + t, t * 4 + u)
        rows = pl.ds(pl.multiple_of(number * GC, GC), GC)
        return kept[rows] + got[rows].astype(F32)

    value = scalars[...] + joined(got[2 * D :])
    own_scalars[...] = value
    parts = three_parts(value)
    lane = lax.broadcasted_iota(jnp.int32, (GC, RW), 1)
    for by, message in enumerate(messages, 1):
        t = lax.rem(mine + by, 4)
        spread = block(t, 3)
        for u in range(3):
            moved = pltpu.roll(spread, RC - u * SPARE, 1)
            message[u * GC : (u + 1) * GC] = jnp.where(lane < RC, block(t, u), moved).astype(BF16)
        message[3 * GC :] = parts
    for u in range(4):
        own[u * GC : (u + 1) * GC] = block(mine, u)


def second_kernel(place, own, scalars, one, two, three, mine, own_scalars, *refs):
    *messages, total = refs
    core, x, y = place[0], place[1], place[2]
    other = jnp.where(core == 0, x, y)
    lane = lax.broadcasted_iota(jnp.int32, (GC, RW), 1)
    spread = jnp.zeros((GC, RW), F32)
    for u in range(3):
        rows = slice(u * GC, (u + 1) * GC)
        came = (one[rows].astype(F32) + two[rows].astype(F32)) + three[rows].astype(F32)
        total[rows] = own[rows] + came
        moved = pltpu.roll(came, (u + 1) * SPARE, 1)
        spread = jnp.where((lane >= u * SPARE) & (lane < (u + 1) * SPARE), moved, spread)
    total[3 * GC :] = own[3 * GC :] + spread

    def block(u):
        return total[pl.ds(pl.multiple_of(u * GC, GC), GC)]

    value = scalars[...]
    for ref in (one, two, three):
        value = value + joined(ref[3 * GC :])
    own_scalars[...] = value
    parts = three_parts(value)
    for by, message in enumerate(messages, 1):
        message[:GC] = block(lax.rem(other + by, 4)).astype(BF16)
        message[GC:] = parts
    mine[...] = block(other)


def third_kernel(own, scalars, one, two, three, turned, own_scalars):
    total = (own[...] + one[:GC].astype(F32)) + (
        two[:GC].astype(F32) + three[:GC].astype(F32)
    )
    value = scalars[...]
    for ref in (one, two, three):
        value = value + joined(ref[GC:])
    own_scalars[...] = value
    turned[...] = total.T[:RC]


def pieces_kernel(img, scalars, own, one, two, three, pieces):
    total = (own[...] + one[:GC].astype(F32)) + (
        two[:GC].astype(F32) + three[:GC].astype(F32)
    )
    both = jnp.concatenate([img[...], total.T[:RC]], axis=1)
    tail = three_parts(scalars[...])[:TAIL, : 2 * GC].astype(F32)
    for i in range(8):
        rows = both[i * PC : (i + 1) * PC]
        pieces[i] = jnp.concatenate([rows, tail], axis=0).astype(BF16)


def last_kernel(got, img, txt, scalars):
    total = got[0].astype(F32)
    for i in range(1, 8):
        total = total + got[i].astype(F32)
    img[...] = total[:PC, :GC]
    txt[...] = total[:PC, GC:]
    scalars[...] = jnp.sum(total[PC:], axis=1, keepdims=True) / COUNT


def first(place, kept, got, scalars):
    own, scalars, *messages = call(
        first_kernel,
        [place, kept, got, scalars],
        [out((4 * GC, RW), F32), out((SV, 1), F32)] + [out((3 * GC + SV, RW), BF16)] * 3,
        0,
        "first",
    )
    return own, scalars, [send(m, first_axis(by)) for by, m in enumerate(messages, 1)]


def second(place, own, scalars, got):
    own, scalars, *messages = call(
        second_kernel,
        [place, own, scalars, *got],
        [out((GC, RW), F32), out((SV, 1), F32)] + [out((GC + SV, RW), BF16)] * 3,
        0,
        "second",
        scratch=[pltpu.VMEM((4 * GC, RW), F32)],
    )
    return own, scalars, [send(m, second_axis(by)) for by, m in enumerate(messages, 1)]


def third(own, scalars, got):
    return call(
        third_kernel,
        [own, scalars, *got],
        [out((RC, GC), F32), out((SV, 1), F32)],
        0,
        "third",
        scalars=0,
    )


def across_z(img, scalars, own, got):
    (pieces,) = call(
        pieces_kernel,
        [img, scalars, own, *got],
        [out((8, PC + TAIL, 2 * GC), BF16)],
        0,
        "pieces",
        scalars=0,
    )
    return call(
        last_kernel,
        [lax.all_to_all(pieces, "z", 0, 0)],
        [out((PC, GC), F32), out((PC, GC), F32), out((TAIL, 1), F32)],
        0,
        "last",
        scalars=0,
    )


def after(done, *values):
    got = lax.optimization_barrier((*values, done))[: len(values)]
    return got[0] if len(values) == 1 else got


def local(img_feats, txt_feats, img_head, txt_head, log_temp, bias):
    core, xh = lax.axis_index("core"), lax.axis_index("xh")
    x = xh * 2 + lax.axis_index("xl")
    place = jnp.stack([core, x, lax.axis_index("y"), xh == core]).astype(jnp.int32)
    scale = jnp.stack([jnp.exp(log_temp), bias])

    feats = after((place, scale), txt_feats)
    t0, txt_unit0, txt_norm0 = embed(feats, txt_head, 0, "embed_t0")
    near_t0 = send(t0, to_partner)
    t1, txt_unit1, txt_norm1, txt = embed(feats, txt_head, CH, "embed_t1", [t0])
    near_t1, sib_t = send(t1, to_partner), send(txt, to_sibling)
    feats = after(t1, img_feats)
    i0, img_unit0, img_norm0 = embed(feats, img_head, 0, "embed_i0")
    near_i0 = send(i0, to_partner)
    i1, img_unit1, img_norm1, img = embed(feats, img_head, CH, "embed_i1", [i0])
    near_i1, sib_i = send(i1, to_partner), send(img, to_sibling)
    txt_unit, txt_norm = [txt_unit0, txt_unit1], [txt_norm0, txt_norm1]
    img_unit, img_norm = [img_unit0, img_unit1], [img_norm0, img_norm1]

    img_rows = ordered(after(img, img_feats))
    txt_rows = ordered(after(img_rows, txt_feats))
    near_t0 = after(txt_rows, near_t0)
    far_t0 = send(near_t0, onward)
    a = pairs(scale, [img], [[near_t0]], None, False, True, "near_a0")
    a = pairs(scale, [img], [[txt], [sib_t]], a, True, True, "own_a")
    (b,) = pairs(after(a[1], scale), [txt], [[img], [sib_i]], None, True, False, "own_b")
    near_t1 = after(b, near_t1)
    far_t1 = send(near_t1, onward)
    a = pairs(scale, [img], [[near_t1, far_t0]], a, False, True, "near_a1")
    chosen_t = choose(after(a[1], place), [near_t0, near_t1], [far_t0, far_t1])
    last_t = send(chosen_t, to_sibling)
    near_i0 = after(a[1], near_i0)
    far_i0 = send(near_i0, onward)
    (b,) = pairs(after(chosen_t, scale), [txt], [[near_i0]], (b,), False, False, "near_b0")
    a = pairs(after(b, scale), [img], [[far_t1]], a, False, True, "far_a")
    near_i1 = after(a[1], near_i1)
    far_i1 = send(near_i1, onward)
    a = pairs(after((a[1], near_i1), scale), [img], [[last_t]], a, False, True, "last_a")
    dz_img, message, scalars = tangent(scale, place, a[0], img_unit, img_norm, img_rows, a[1])
    got = send(message, to_sibling)
    (b,) = pairs(after(dz_img, scale), [txt], [[near_i1, far_i0]], (b,), False, False, "near_b1")
    kept = keep(after(b, place), dz_img, img_rows, "keep_img")
    kept_img = kept
    chosen_i = choose(after(kept, place), [near_i0, near_i1], [far_i0, far_i1])
    last_i = send(chosen_i, to_sibling)
    (b,) = pairs(after(chosen_i, scale), [txt], [[far_i1]], (b,), False, False, "far_b")
    (b,) = pairs(scale, [txt], [[last_i]], (b,), False, False, "last_b")
    none = jnp.zeros((8, ROWS), F32)
    dz_txt, message, no_scalars = tangent(scale, place, b, txt_unit, txt_norm, txt_rows, none)
    got_txt = send(message, to_sibling)
    own, scalars, got = first(after(dz_txt, place), kept_img, got, scalars)
    kept = keep(after(own, place), dz_txt, txt_rows, "keep_txt")
    own_txt, no_scalars, got_txt = first(place, kept, got_txt, no_scalars)
    grad_txt_feats = back(after(own_txt, dz_txt), txt_head, "back_txt")
    own, scalars, got = second(after(grad_txt_feats, place), own, scalars, got)
    own_x, no_scalars, got_x = second(after(own, place), own_txt, no_scalars, got_txt)
    img_turned, scalars = third(after(own_x, own), scalars, got)
    grad_img_feats = back(after(img_turned, dz_img), img_head, "back_img")
    own, got = after(grad_img_feats, own_x), got_x
    grad_img_head, grad_txt_head, scalars = across_z(img_turned, scalars, own, got)
    loss, grad_bias, grad_log_temp = (scalars[i, 0] for i in range(3))
    return (
        loss,
        grad_log_temp,
        grad_bias,
        grad_img_feats,
        grad_txt_feats,
        grad_img_head,
        grad_txt_head,
    )


def solution(mesh):
    fine = Mesh(mesh.devices.reshape(SIZES), AXES)
    rows = P(AXES, None)
    tile = P(AXES[:3], AXES[3:])
    return jax.shard_map(
        local,
        mesh=fine,
        in_specs=(rows, rows, P(), P(), P(), P()),
        out_specs=(P(), P(), P(), rows, rows, tile, tile),
        check_vma=False,
    )
```

```python
import functools

import jax
import jax.numpy as jnp
import numpy as np
from jax import lax
from jax.experimental import pallas as pl
from jax.experimental.pallas import tpu as pltpu
from jax.sharding import Mesh
from jax.sharding import PartitionSpec as P

AXES = ("z", "xh", "core", "xl", "y")
SIZES = (8, 2, 2, 2, 4)
ROUNDS = 2
ORDER = (2, 1, 3)
TAIL = 4
ROWS = 448
D = 1152
CHUNKS = 2
CH = ROWS // CHUNKS
GC = 144
RC = 288
SPARE = 96
RW = 384
PC = 36
SV = 16
COUNT = 256 * ROWS * ROWS * (2 * ROUNDS + 1)
COST = {"own_a": 30, "own_b": 30, "near_b0": 30, "keep_img": 30, "keep_txt": 16}
F32 = jnp.float32
BF16 = jnp.bfloat16
NT = (((1,), (1,)), ((), ()))
TN = (((0,), (0,)), ((), ()))


def permutation(move):
    pairs = []
    for source in range(int(np.prod(SIZES))):
        z, xh, core, xl, y = (int(i) for i in np.unravel_index(source, SIZES))
        place = {"z": z, "x": xh * 2 + xl, "y": y, "core": core}
        place = {**place, **move(place)}
        x = place["x"] % 4
        target = (place["z"] % 8, x // 2, place["core"] % 2, x % 2, place["y"] % 4)
        pairs.append((source, int(np.ravel_multi_index(target, SIZES))))
    return pairs


def send(value, move):
    return lax.ppermute(value, AXES, permutation(move))


def to_partner(p):
    return {"x": p["x"] + 2}


def onward(p):
    return {"z": p["z"] + (1 if p["x"] < 2 else -1)}


def to_sibling(p):
    return {"core": p["core"] + 1}


def first_axis(by):
    return lambda p: {"y": p["y"] + by} if p["core"] == 0 else {"x": p["x"] + by}


def second_axis(by):
    return lambda p: {"x": p["x"] + by} if p["core"] == 0 else {"y": p["y"] + by}


VMEM = pl.BlockSpec(memory_space=pltpu.VMEM)
SMEM = pl.BlockSpec(memory_space=pltpu.SMEM)


def call(kernel, inputs, outputs, flops, name, scalars=1, limit=24, scratch=()):
    size = sum(int(np.prod(a.shape)) * a.dtype.itemsize for a in [*inputs, *outputs])
    return pl.pallas_call(
        kernel,
        out_shape=tuple(outputs),
        in_specs=[SMEM] * scalars + [VMEM] * (len(inputs) - scalars),
        out_specs=tuple(VMEM for _ in outputs),
        scratch_shapes=scratch,
        compiler_params=pltpu.CompilerParams(vmem_limit_bytes=limit * 1024 * 1024),
        cost_estimate=pl.CostEstimate(flops=COST.get(name, 0) * 10**9, bytes_accessed=0, transcendentals=0),
        name=name,
    )(*inputs)


def out(shape, dtype):
    return jax.ShapeDtypeStruct(shape, dtype)


def embed_kernel(start, feats, head, *refs):
    z = jnp.dot(feats[start : start + CH], head[...], preferred_element_type=F32)
    n = jnp.sqrt(jnp.sum(z * z, axis=-1, keepdims=True) + 1e-06)
    e = z * (1.0 / n)
    low = e.astype(BF16)
    emb, unit, norm = refs[-3:] if start == 0 else refs[1:4]
    unit[...] = e
    norm[...] = n
    emb[...] = low
    if start:
        refs[4][:start] = refs[0][...]
        refs[4][start:] = low


def embed(feats, head, start, name, earlier=()):
    shapes = [out((CH, D), BF16), out((CH, D), F32), out((CH, 1), F32)]
    return call(
        functools.partial(embed_kernel, start),
        [feats, head, *earlier],
        shapes + [out((ROWS, D), BF16)] * len(earlier),
        2 * CH * D * D,
        name,
        scalars=0,
    )


def whole(refs):
    values = [r[...] for r in refs]
    return values[0] if len(values) == 1 else jnp.concatenate(values, axis=0)


def pair_kernel(rows_in, blocks, own, stats, more, *refs):
    refs = list(refs)
    scale = refs.pop(0)
    rows = whole([refs.pop(0) for _ in range(rows_in)])
    cols = [[refs.pop(0) for _ in range(n)] for n in blocks]
    before = [refs.pop(0) for _ in range((2 if stats else 1) if more else 0)]
    total_out = refs.pop(0)
    temp, bias = scale[0], scale[1]
    total = before[0][...] if more else None
    sums = before[1][...] if more and stats else None
    for i, group in enumerate(cols):
        block = whole(group)
        scaled = temp * lax.dot_general(rows, block, NT, preferred_element_type=F32)
        logits = scaled + bias
        small = jnp.exp(-jnp.abs(logits))
        inverse = 1.0 / (1.0 + small)
        grads = jnp.where(logits >= 0, inverse, small * inverse)
        mark = None
        if own and i == 0:
            shape = logits.shape
            mark = lax.broadcasted_iota(jnp.int32, shape, 0) == lax.broadcasted_iota(
                jnp.int32, shape, 1
            )
            grads = jnp.where(mark, grads - 1.0, grads)
        if stats:
            signed = logits if mark is None else jnp.where(mark, -logits, logits)
            terms = jnp.maximum(signed, 0.0) + jnp.log1p(small)
            width = logits.shape[1]
            three = [
                jnp.sum(v, axis=0, keepdims=True) for v in (terms, grads, grads * scaled)
            ]
            tile = jnp.concatenate([*three, jnp.zeros((5, width), F32)], axis=0)
            if width < ROWS:
                tile = jnp.concatenate([tile, jnp.zeros((8, ROWS - width), F32)], axis=1)
            sums = tile if sums is None else sums + tile
        part = jnp.dot(grads.astype(BF16), block, preferred_element_type=F32)
        total = part if total is None else total + part
    total_out[...] = total
    if stats:
        refs[0][...] = sums


def pairs(scale, emb, cols, state, own, stats, name):
    n = sum(c.shape[0] for group in cols for c in group)
    got = call(
        functools.partial(
            pair_kernel, len(emb), [len(g) for g in cols], own, stats, state is not None
        ),
        [scale, *emb, *(c for group in cols for c in group), *(state or ())],
        [out((ROWS, D), F32)] + ([out((8, ROWS), F32)] if stats else []),
        4 * ROWS * n * D,
        name,
    )
    return tuple(got)


def choose_kernel(place, *refs):
    chosen = refs[-1]

    @pl.when(place[3] == 1)
    def _():
        for i in range(CHUNKS):
            chosen[i * CH : (i + 1) * CH] = refs[i][...]

    @pl.when(place[3] == 0)
    def _():
        for i in range(CHUNKS):
            chosen[i * CH : (i + 1) * CH] = refs[CHUNKS + i][...]


def choose(place, near, far):
    return call(choose_kernel, [place, *near, *far], [out((ROWS, D), BF16)], 0, "choose")[0]


def order_kernel(feats, rows):
    values = feats[...]
    row = lax.broadcasted_iota(jnp.int32, (D, RW), 0)
    col = lax.broadcasted_iota(jnp.int32, (D, RW), 1)
    wanted = jnp.where(col < RC, col + lax.div(col, PC) * (3 * PC), -D)
    for c in range(2):
        for h in range(2):
            pick = (row == wanted + (c * PC + h * 2 * PC)).astype(F32).astype(BF16)
            rows[c * 2 + h] = jnp.dot(values, pick, preferred_element_type=F32).astype(BF16)


def ordered(feats):
    return call(
        order_kernel, [feats], [out((4, ROWS, RW), BF16)], 2 * ROWS * D * D, "ordered", scalars=0
    )[0]


def three_parts(value):
    high = value.astype(BF16).astype(F32)
    rest = value - high
    middle = rest.astype(BF16).astype(F32)
    lane = lax.broadcasted_iota(jnp.int32, (SV, RW), 1)
    parts = jnp.where(lane == 0, high, jnp.where(lane == 1, middle, jnp.where(lane == 2, rest - middle, 0.0)))
    return parts.astype(BF16)


def joined(rows):
    return jnp.sum(rows.astype(F32), axis=1, keepdims=True)


def tangent_kernel(scale, place, total, unit0, unit1, norm0, norm1, feats, sums, dz, message, scalars):
    core = place[0]
    lows = []
    for i, (unit, norm) in enumerate(((unit0, norm0), (unit1, norm1))):
        grad = scale[0] * total[i * CH : (i + 1) * CH]
        e = unit[...]
        along = jnp.sum(e * grad, axis=-1, keepdims=True)
        lows.append(((grad - e * along) * (1.0 / norm[...])).astype(BF16))
    low = jnp.concatenate(lows, axis=0)
    dz[...] = low
    for half in range(2):
        part = lax.dot_general(low, feats[(1 - core) * 2 + half], TN, preferred_element_type=F32)
        message[half * D : (half + 1) * D] = part.astype(BF16)
    value = jnp.sum(sums[...], axis=1, keepdims=True)
    value = jnp.concatenate([value, jnp.zeros((SV - 8, 1), F32)], axis=0)
    scalars[...] = value
    message[2 * D :] = three_parts(value)


def tangent(scale, place, total, unit, norm, feats, sums):
    return call(
        tangent_kernel,
        [scale, place, total, *unit, *norm, feats, sums],
        [out((ROWS, D), BF16), out((2 * D + SV, RW), BF16), out((SV, 1), F32)],
        2 * ROWS * D * D // 2,
        "tangent",
        scalars=2,
    )


def keep_kernel(place, dz, feats, kept):
    core = place[0]
    for half in range(2):
        kept[half * D : (half + 1) * D] = lax.dot_general(
            dz[...], feats[core * 2 + half], TN, preferred_element_type=F32
        )


def keep(place, dz, feats, name):
    return call(keep_kernel, [place, dz, feats], [out((2 * D, RW), F32)], ROWS * D * D, name)[0]


def back_kernel(dz, head, grad):
    grad[...] = lax.dot_general(dz[...], head[...], NT, preferred_element_type=F32).astype(BF16)


def back(dz, head, name):
    return call(
        back_kernel, [dz, head], [out((ROWS, D), BF16)], 2 * ROWS * D * D, name, scalars=0
    )[0]


def first_kernel(place, kept, got, scalars, own, own_scalars, *messages):
    core, x, y = place[0], place[1], place[2]
    mine = jnp.where(core == 0, y, x)

    def block(t, u):
        number = jnp.where(core == 0, u * 4 + t, t * 4 + u)
        rows = pl.ds(pl.multiple_of(number * GC, GC), GC)
        return kept[rows] + got[rows].astype(F32)

    value = scalars[...] + joined(got[2 * D :])
    own_scalars[...] = value
    parts = three_parts(value)
    lane = lax.broadcasted_iota(jnp.int32, (GC, RW), 1)
    for by, message in zip(ORDER, messages, strict=True):
        t = lax.rem(mine + by, 4)
        spread = block(t, 3)
        for u in range(3):
            moved = pltpu.roll(spread, RC - u * SPARE, 1)
            message[u * GC : (u + 1) * GC] = jnp.where(lane < RC, block(t, u), moved).astype(BF16)
        message[3 * GC :] = parts
    for u in range(4):
        own[u * GC : (u + 1) * GC] = block(mine, u)


def second_kernel(place, own, scalars, one, two, three, mine, own_scalars, *refs):
    *messages, total = refs
    core, x, y = place[0], place[1], place[2]
    other = jnp.where(core == 0, x, y)
    lane = lax.broadcasted_iota(jnp.int32, (GC, RW), 1)
    spread = jnp.zeros((GC, RW), F32)
    for u in range(3):
        rows = slice(u * GC, (u + 1) * GC)
        came = (one[rows].astype(F32) + two[rows].astype(F32)) + three[rows].astype(F32)
        total[rows] = own[rows] + came
        moved = pltpu.roll(came, (u + 1) * SPARE, 1)
        spread = jnp.where((lane >= u * SPARE) & (lane < (u + 1) * SPARE), moved, spread)
    total[3 * GC :] = own[3 * GC :] + spread

    def block(u):
        return total[pl.ds(pl.multiple_of(u * GC, GC), GC)]

    value = scalars[...]
    for ref in (one, two, three):
        value = value + joined(ref[3 * GC :])
    own_scalars[...] = value
    parts = three_parts(value)
    for by, message in zip(ORDER, messages, strict=True):
        message[:GC] = block(lax.rem(other + by, 4)).astype(BF16)
        message[GC:] = parts
    mine[...] = block(other)


def third_kernel(own, scalars, one, two, three, turned, own_scalars):
    total = (own[...] + one[:GC].astype(F32)) + (
        two[:GC].astype(F32) + three[:GC].astype(F32)
    )
    value = scalars[...]
    for ref in (one, two, three):
        value = value + joined(ref[GC:])
    own_scalars[...] = value
    turned[...] = total.T[:RC]


def pieces_kernel(img, scalars, own, one, two, three, pieces):
    total = (own[...] + one[:GC].astype(F32)) + (
        two[:GC].astype(F32) + three[:GC].astype(F32)
    )
    both = jnp.concatenate([img[...], total.T[:RC]], axis=1)
    tail = three_parts(scalars[...])[:TAIL, : 2 * GC].astype(F32)
    for i in range(8):
        rows = both[i * PC : (i + 1) * PC]
        pieces[i] = jnp.concatenate([rows, tail], axis=0).astype(BF16)


def last_kernel(got, img, txt, scalars):
    total = got[0].astype(F32)
    for i in range(1, 8):
        total = total + got[i].astype(F32)
    img[...] = total[:PC, :GC]
    txt[...] = total[:PC, GC:]
    scalars[...] = jnp.sum(total[PC:], axis=1, keepdims=True) / COUNT


def first(place, kept, got, scalars):
    own, scalars, *messages = call(
        first_kernel,
        [place, kept, got, scalars],
        [out((4 * GC, RW), F32), out((SV, 1), F32)] + [out((3 * GC + SV, RW), BF16)] * 3,
        0,
        "first",
    )
    return own, scalars, [send(m, first_axis(by)) for by, m in zip(ORDER, messages, strict=True)]


def second(place, own, scalars, got):
    own, scalars, *messages = call(
        second_kernel,
        [place, own, scalars, *got],
        [out((GC, RW), F32), out((SV, 1), F32)] + [out((GC + SV, RW), BF16)] * 3,
        0,
        "second",
        scratch=[pltpu.VMEM((4 * GC, RW), F32)],
    )
    return own, scalars, [send(m, second_axis(by)) for by, m in zip(ORDER, messages, strict=True)]


def third(own, scalars, got):
    return call(
        third_kernel,
        [own, scalars, *got],
        [out((RC, GC), F32), out((SV, 1), F32)],
        0,
        "third",
        scalars=0,
    )


def across_z(img, scalars, own, got):
    (pieces,) = call(
        pieces_kernel,
        [img, scalars, own, *got],
        [out((8, PC + TAIL, 2 * GC), BF16)],
        0,
        "pieces",
        scalars=0,
    )
    return call(
        last_kernel,
        [lax.all_to_all(pieces, "z", 0, 0)],
        [out((PC, GC), F32), out((PC, GC), F32), out((TAIL, 1), F32)],
        0,
        "last",
        scalars=0,
    )


def after(done, *values):
    got = lax.optimization_barrier((*values, done))[: len(values)]
    return got[0] if len(values) == 1 else got


def local(img_feats, txt_feats, img_head, txt_head, log_temp, bias):
    core, xh = lax.axis_index("core"), lax.axis_index("xh")
    x = xh * 2 + lax.axis_index("xl")
    place = jnp.stack([core, x, lax.axis_index("y"), xh == core]).astype(jnp.int32)
    scale = jnp.stack([jnp.exp(log_temp), bias])

    feats = after((place, scale), txt_feats)
    t0, txt_unit0, txt_norm0 = embed(feats, txt_head, 0, "embed_t0")
    near_t0 = send(t0, to_partner)
    t1, txt_unit1, txt_norm1, txt = embed(feats, txt_head, CH, "embed_t1", [t0])
    near_t1, sib_t = send(t1, to_partner), send(txt, to_sibling)
    feats = after(t1, img_feats)
    i0, img_unit0, img_norm0 = embed(feats, img_head, 0, "embed_i0")
    near_i0 = send(i0, to_partner)
    i1, img_unit1, img_norm1, img = embed(feats, img_head, CH, "embed_i1", [i0])
    near_i1, sib_i = send(i1, to_partner), send(img, to_sibling)
    txt_unit, txt_norm = [txt_unit0, txt_unit1], [txt_norm0, txt_norm1]
    img_unit, img_norm = [img_unit0, img_unit1], [img_norm0, img_norm1]

    img_rows = ordered(after(img, img_feats))
    txt_rows = ordered(after(img_rows, txt_feats))
    near_t0 = after(txt_rows, near_t0)
    far_t0 = send(near_t0, onward)
    a = pairs(scale, [img], [[near_t0]], None, False, True, "near_a0")
    a = pairs(scale, [img], [[txt], [sib_t]], a, True, True, "own_a")
    (b,) = pairs(after(a[1], scale), [txt], [[img], [sib_i]], None, True, False, "own_b")
    near_t1 = after(b, near_t1)
    far_t1 = send(near_t1, onward)
    a = pairs(scale, [img], [[near_t1, far_t0]], a, False, True, "near_a1")
    chosen_t = choose(after(a[1], place), [near_t0, near_t1], [far_t0, far_t1])
    last_t = send(chosen_t, to_sibling)
    near_i0 = after(a[1], near_i0)
    far_i0 = send(near_i0, onward)
    (b,) = pairs(after(chosen_t, scale), [txt], [[near_i0]], (b,), False, False, "near_b0")
    a = pairs(after(b, scale), [img], [[far_t1]], a, False, True, "far_a")
    near_i1 = after(a[1], near_i1)
    far_i1 = send(near_i1, onward)
    a = pairs(after((a[1], near_i1), scale), [img], [[last_t]], a, False, True, "last_a")
    dz_img, message, scalars = tangent(scale, place, a[0], img_unit, img_norm, img_rows, a[1])
    got = send(message, to_sibling)
    (b,) = pairs(after(dz_img, scale), [txt], [[near_i1, far_i0]], (b,), False, False, "near_b1")
    kept = keep(after(b, place), dz_img, img_rows, "keep_img")
    kept_img = kept
    chosen_i = choose(after(kept, place), [near_i0, near_i1], [far_i0, far_i1])
    last_i = send(chosen_i, to_sibling)
    (b,) = pairs(after(chosen_i, scale), [txt], [[far_i1]], (b,), False, False, "far_b")
    (b,) = pairs(scale, [txt], [[last_i]], (b,), False, False, "last_b")
    none = jnp.zeros((8, ROWS), F32)
    dz_txt, message, no_scalars = tangent(scale, place, b, txt_unit, txt_norm, txt_rows, none)
    got_txt = send(message, to_sibling)
    own, scalars, got = first(after(dz_txt, place), kept_img, got, scalars)
    kept = keep(after(own, place), dz_txt, txt_rows, "keep_txt")
    own_txt, no_scalars, got_txt = first(place, kept, got_txt, no_scalars)
    grad_txt_feats = back(after(own_txt, dz_txt), txt_head, "back_txt")
    own, scalars, got = second(after(grad_txt_feats, place), own, scalars, got)
    own_x, no_scalars, got_x = second(after(own, place), own_txt, no_scalars, got_txt)
    img_turned, scalars = third(after(own_x, own), scalars, got)
    grad_img_feats = back(after(img_turned, dz_img), img_head, "back_img")
    own, got = after(grad_img_feats, own_x), got_x
    grad_img_head, grad_txt_head, scalars = across_z(img_turned, scalars, own, got)
    loss, grad_bias, grad_log_temp = (scalars[i, 0] for i in range(3))
    return (
        loss,
        grad_log_temp,
        grad_bias,
        grad_img_feats,
        grad_txt_feats,
        grad_img_head,
        grad_txt_head,
    )


def solution(mesh):
    fine = Mesh(mesh.devices.reshape(SIZES), AXES)
    rows = P(AXES, None)
    tile = P(AXES[:3], AXES[3:])
    return jax.shard_map(
        local,
        mesh=fine,
        in_specs=(rows, rows, P(), P(), P(), P()),
        out_specs=(P(), P(), P(), rows, rows, tile, tile),
        check_vma=False,
    )
```
